512 devices in a mesh: doc: 16 (over x, z_hi), samp: 8 (over y), tok: 4 (over z_lo, core).
Axes of the slice: x: 4, y: 8, z: 8 (z_hi: 4, z_lo: 2; z = z_hi * 2 + z_lo), core: 2. Of those that a mesh axis runs over, the one named last changes fastest.
Arguments:
- context: bfloat16 [512, 128, 1024], P(('doc', 'samp', 'tok')), parts along dimension 0, may hold values from -6 to 6
- hidden: bfloat16 [512, 128, 1024], P(('doc', 'samp', 'tok')), parts along dimension 0, may hold values from -12 to 12
- out_weight: bfloat16 [1024, 1024], P(None, ('samp', 'tok')), may hold values from -0.1875 to 0.1875
- out_bias: float32 [1024], replicated, may hold values from -3 to 3
- norm_gain: float32 [1024], replicated, may hold values from 0.5 to 1.5
- norm_bias: float32 [1024], replicated, may hold values from -2 to 2
- token_ids: int32 [512, 128], P(('doc', 'samp', 'tok')), parts along dimension 0, may hold values from 0 to 50264
- lengths: int32 [512], P(('doc', 'samp', 'tok')), parts along dimension 0, may hold values from 32 to 128, as said below
- idf_table: bfloat16 [50265], replicated, may hold values from 1 to 12
Outputs:
- embeddings: bfloat16 [512, 128, 1024], P(('doc', 'samp', 'tok')), parts along dimension 0
- precision: float32 [512, 32], P(('doc', 'samp', 'tok')), parts along dimension 0
- recall: float32 [512, 32], P(('doc', 'samp', 'tok')), parts along dimension 0
- f_score: float32 [512, 32], P(('doc', 'samp', 'tok')), parts along dimension 0
- utility: float32 [512], P(('doc', 'samp', 'tok')), parts along dimension 0
The draws below stay inside these ranges and needn't reach their ends.
There are 16 independent parts, one for each index of `doc`. The reference program is written for one: setup_inputs(seed, part) draws one part's arguments, and reference() takes and returns one part's arrays. A program takes and returns all parts, laid end to end along the dimension named above; an argument that names none is the same for every part. Nothing has to cross between parts.
Inputs may be any that keep to these rules, and one draw needn't show every extreme that they name: `lengths`: in every document some summary has all 128 tokens real.
All inputs are finite; a program needn't handle non-finite values.
Results may differ from the reference program's by a relative error of at most 0.001.
Values may be sent and summed in bfloat16 or wider, within the bound.
A program may use at most 64 MiB of HBM per device.

```python
import math
import jax
import jax.numpy as jnp
import numpy as np
from jax import lax

D = 1024
VOCAB = 50265
SEQ = 128
SAMPLES = 32


def draw_lengths(key, part):
    key = jax.random.fold_in(key, 11)
    first_key, second_key = jax.random.split(key)
    counts = jax.random.randint(first_key, (SAMPLES,), SEQ // 4, SEQ + 1)
    chosen = jax.random.randint(second_key, (), 0, SAMPLES)
    return jnp.where(jnp.arange(SAMPLES) == chosen, SEQ, counts).astype(jnp.int32)


def draw_hidden(key, part):
    key = jax.random.fold_in(key, 5)
    dir_key, sign_key, size_key, noise_key = jax.random.split(key, 4)
    direction = jax.random.truncated_normal(dir_key, -4.0, 4.0, (D,), jnp.float32)
    order = jax.random.permutation(sign_key, SAMPLES)
    signs = jnp.where(order < SAMPLES // 2, 1.0, -1.0).astype(jnp.float32)
    sizes_drawn = jax.random.uniform(size_key, (SAMPLES,), jnp.float32, 0.5, 2.0)
    noise = jax.random.truncated_normal(noise_key, -4.0, 4.0, (SAMPLES, SEQ, D), jnp.float32)
    amplitude = signs * sizes_drawn
    values = noise + amplitude[:, None, None] * direction[None, None, :]
    return values.astype(jnp.bfloat16)


def with_ends(array, rng, smallest, high):
    longest = array.shape.index(max(array.shape))
    spots = []
    for shift in (0, 1):
        where = [jax.random.randint(jax.random.fold_in(rng, axis), (), 0, length) for axis, length in enumerate(array.shape)]
        where[longest] = (where[longest] + shift) % array.shape[longest]
        spots.append(tuple(where))
    return array.at[spots[0]].set(smallest).at[spots[1]].set(high)


def level_of(stream_key, shape, pieces, smallest, largest):
    level = 1.0
    for position, blocks in pieces:
        draws = jax.random.uniform(jax.random.fold_in(jax.random.fold_in(stream_key, 6), position), (blocks,), jnp.float32, smallest / len(pieces), largest / len(pieces))
        level = level * jnp.repeat(jnp.exp(draws), shape[position] // blocks).reshape((-1,) + (1,) * (len(shape) - 1 - position))
    return level


def rank_bounds(number_of, skew):
    portions = [(1 << 20) // math.isqrt(standing ** skew) + 1 for standing in range(1, number_of + 1)]
    scale = 1 + sum(portions) // (1 << 30)
    return np.cumsum(np.array([max(1, weight // scale) for weight in portions]))


def skewed_ids(key, extent, count, slope):
    table = rank_bounds(count, slope)
    ticket = jax.random.randint(jax.random.fold_in(key, 1), extent, 0, int(table[count - 1]))
    rank = jnp.searchsorted(jnp.asarray(table, jnp.int32), ticket, side="right")
    return jax.random.permutation(jax.random.fold_in(key, 2), count)[rank].astype(jnp.int32)


def bell_draw(key, extent, deviation, bound, pieces=(), kind=jnp.bfloat16):
    array = deviation * jax.random.normal(key, extent, jnp.float32)
    if pieces:
        array = array * level_of(key, extent, pieces, -0.22, 0.18)
    return jnp.clip(array, -bound, bound).astype(kind)


def setup_inputs(seed: int = 0, part: int = 0) -> dict:
    streams_of = jax.random.split(jax.random.key(seed), 10)
    part_keys = jax.random.split(jax.random.fold_in(streams_of[9], part), 10)
    context = bell_draw(part_keys[0], (SAMPLES, SEQ, D), 1.0, 6.0, ((0, 32),))
    hidden = draw_hidden(jax.random.fold_in(jax.random.fold_in(streams_of[9], part), 71), part)
    out_weight = bell_draw(streams_of[2], (D, D), D ** -0.5, 0.1875, ((1, 32),))
    out_bias = bell_draw(streams_of[3], (D,), 0.5, 3.0, (), jnp.float32)
    norm_gain = jnp.clip(1.0 + 0.1 * jax.random.normal(streams_of[4], (D,), jnp.float32), 0.5, 1.5)
    norm_bias = bell_draw(streams_of[5], (D,), 0.3, 2.0, (), jnp.float32)
    token_ids = with_ends(skewed_ids(part_keys[6], (SAMPLES, SEQ), VOCAB, 2), jax.random.fold_in(part_keys[6], 3), 0, VOCAB - 1).astype(jnp.int32)
    lengths = draw_lengths(jax.random.fold_in(jax.random.fold_in(streams_of[9], part), 71), part)
    idf_table = jnp.clip(jnp.exp(jax.random.uniform(streams_of[8], (VOCAB,), jnp.float32, math.log(1.0), math.log(12.0))), 1.0, 12.0).astype(jnp.bfloat16)
    return dict(context=context, hidden=hidden, out_weight=out_weight, out_bias=out_bias, norm_gain=norm_gain, norm_bias=norm_bias, token_ids=token_ids, lengths=lengths, idf_table=idf_table)


def reference(context, hidden, out_weight, out_bias, norm_gain, norm_bias, token_ids, lengths, idf_table):
    flat_ctx = context.reshape(SAMPLES * SEQ, D)
    pre = jnp.dot(flat_ctx, out_weight, preferred_element_type=jnp.float32)
    mixed = hidden.reshape(SAMPLES * SEQ, D).astype(jnp.float32) + pre + out_bias
    centre = mixed - lax.optimization_barrier(jnp.mean(mixed, axis=-1, keepdims=True))
    spread = lax.optimization_barrier(jnp.mean(centre * centre, axis=-1, keepdims=True))
    embedded = (centre * lax.rsqrt(spread + 1e-07) * norm_gain + norm_bias).astype(jnp.bfloat16)
    values = embedded.astype(jnp.float32)
    units = (values * lax.rsqrt(lax.optimization_barrier(jnp.sum(values * values, axis=-1, keepdims=True)) + 1e-06)).astype(jnp.bfloat16)
    units = units.reshape(SAMPLES, SEQ, D)
    positions = jnp.arange(SEQ, dtype=jnp.int32)
    valid = positions[None, :] < lengths[:, None]
    weights = jnp.where(valid, idf_table[token_ids].astype(jnp.float32), 0.0)
    precision_rows = []
    recall_rows = []
    for first in range(SAMPLES):

        def against(other):
            sim = jnp.dot(units[first], units[other].T, preferred_element_type=jnp.float32)
            both = valid[first][:, None] & valid[other][None, :]
            masked = jnp.where(both, sim, -3.0)
            prec = jnp.sum(weights[first] * lax.optimization_barrier(jnp.max(masked, axis=1))) / jnp.sum(weights[first])
            rec = jnp.sum(weights[other] * lax.optimization_barrier(jnp.max(masked, axis=0))) / jnp.sum(weights[other])
            return (prec, rec)
        prec_row, rec_row = lax.map(against, jnp.arange(SAMPLES, dtype=jnp.int32))
        precision_rows.append(prec_row)
        recall_rows.append(rec_row)
    precision = jnp.stack(precision_rows)
    recall = jnp.stack(recall_rows)
    f_score = 2.0 * precision * recall / jnp.maximum(precision + recall, 0.25)
    utility = (lax.optimization_barrier(jnp.sum(f_score, axis=1)) - jnp.diagonal(f_score)) / (SAMPLES - 1)
    return (embedded.reshape(SAMPLES, SEQ, D), precision, recall, f_score, utility)
```

```python
import jax
import jax.numpy as jnp
from jax import lax
from jax.experimental import pallas as pl
from jax.experimental.pallas import tpu as pltpu
from jax.sharding import PartitionSpec as P

MESH = pl.DeviceIdType.MESH
F32 = jnp.float32
BF16 = jnp.bfloat16

SEQ = 128
WIDTH = 1024
RING = 8
SLICE = 32
SLOTS = 4
PIECE = 16
PIECES = 2 * SLICE // PIECE
CHUNKS = 4
ROWS = SEQ // CHUNKS
NT = (((1,), (1,)), ((), ()))

OWN, M1, M2, P1, C1, P2, C2 = range(7)
PLACES = {OWN: (0, 0), M1: (-1, 0), M2: (-2, 0), P1: (1, 0), C1: (1, 1), P2: (2, 0), C2: (2, 1)}
USED = [(OWN, 1), (M1, 0), (M1, 1), (M2, 0), (M2, 1), (P1, 0), (P1, 1), (C1, 0), (P2, 0), (C2, 0)]


def kernel(
    context_hbm, hidden_hbm, weight_hbm, bias_hbm, gain_hbm, shift_hbm, ids_hbm, length_hbm, table_hbm,
    embedded_out, scores_out,
    ctx, hid, wt, part, mixed, params, ids_ref, length_ref, flat, table, units, first_unit, tokw, result, arrived,
    load_sem, first_sem, chain_send, z_send, ctx_send, part_send, tokw_send, unit_send, result_send,
    slice_sem, z_sem, ctx_sem, part_sem, tokw_sem, unit_sem, result_sem,
):
    doc = lax.axis_index("doc")
    y = lax.axis_index("samp")
    tok = lax.axis_index("tok")
    z, c = tok // 2, tok % 2

    def device(dy, flip_z, flip_c):
        yy = (y + dy + RING) % RING
        zz = 1 - z if flip_z else z
        cc = 1 - c if flip_c else c
        return (doc, yy, zz * 2 + cc)

    def number(blk, s):
        dy = jnp.where(blk <= M2, -blk, (blk - 1) // 2)
        flip = jnp.where((blk == C1) | (blk == C2), 1, 0)
        return (y + dy + RING) % RING * 4 + (z + flip) % 2 * 2 + (c + s) % 2

    up, down, inner, mate = device(1, 0, 0), device(-1, 0, 0), device(0, 1, 0), device(0, 0, 1)
    ahead = device(1 - 2 * c, 0, 0)

    def rows_of(zz, piece):
        return pl.ds(pl.multiple_of(zz * 2 * SLICE + piece * PIECE, PIECE), PIECE)

    def own_piece(h):
        return weight_hbm.at[pl.ds(h * PIECE, PIECE)], wt.at[0, rows_of(z, c * 2 + h)]

    @pl.when(c == 0)
    def _():
        for h in (0, 1):
            pltpu.make_async_copy(*own_piece(h), slice_sem.at[0, h]).start()

    loads = [
        pltpu.make_async_copy(context_hbm.at[0], ctx.at[0], load_sem.at[0]),
        pltpu.make_async_copy(table_hbm, flat, load_sem.at[1]),
        pltpu.make_async_copy(ids_hbm, ids_ref, load_sem.at[2]),
        pltpu.make_async_copy(length_hbm, length_ref, load_sem.at[3]),
        pltpu.make_async_copy(hidden_hbm.at[0], hid, load_sem.at[4]),
        pltpu.make_async_copy(bias_hbm, params.at[0], load_sem.at[5]),
        pltpu.make_async_copy(gain_hbm, params.at[1], load_sem.at[6]),
        pltpu.make_async_copy(shift_hbm, params.at[2], load_sem.at[7]),
    ]
    for load in loads:
        load.start()

    partners = [inner, mate]
    partners += [device(dy, 0, fc) for dy in (1, -1, 2, -2) for fc in (0, 1)]
    partners += [device(dy, 1, 0) for dy in (1, -1, 2, -2)]
    barrier = pltpu.get_barrier_semaphore()
    for partner in partners:
        pl.semaphore_signal(barrier, inc=1, device_id=partner, device_id_type=MESH)

    def remote(src, dst, send_sem, recv_sem, target):
        return pltpu.make_async_remote_copy(
            src_ref=src, dst_ref=dst, send_sem=send_sem, recv_sem=recv_sem,
            device_id=target, device_id_type=MESH,
        )

    def landed(dst, recv_sem):
        remote(dst, dst, ctx_send, recv_sem, mate).wait_recv()

    def sent(src, send_sem):
        remote(src, src, send_sem, ctx_sem, mate).wait_send()

    result[...] = jnp.zeros_like(result)
    pl.semaphore_wait(barrier, len(partners))

    below = (doc, (y + RING - 1) % RING, z * 2 + 1)

    for h in (0, 1):
        @pl.when(c == 0)
        def _(h=h):
            remote(*own_piece(h), first_sem.at[1, h], slice_sem.at[0, h], below).start()

        @pl.when(c == 1)
        def _(h=h):
            remote(*own_piece(h), first_sem.at[1, h], slice_sem.at[0, 2 + h], below).start()
            remote(*own_piece(h), first_sem.at[0, h], slice_sem.at[0, 2 + h], mate).start()

    loads[0].wait()
    remote(ctx.at[0], ctx.at[1], ctx_send, ctx_sem, mate).start()

    def columns_at(k, core):
        yy = (y + RING + jnp.where(core == 0, -k, k + 1)) % RING
        return pl.ds(pl.multiple_of(yy * SEQ, SEQ), SEQ)

    lane = lax.broadcasted_iota(jnp.int32, (1, SEQ), 1)

    def token_weights():
        for load in loads[1:4]:
            load.wait()
        vocab = flat.shape[0]
        full = vocab // WIDTH
        table[pl.ds(full * 8, 16)] = jnp.zeros((16, SEQ), BF16)

        @pl.loop(0, full)
        def _(k):
            table[pl.ds(pl.multiple_of(k * 8, 8), 8)] = flat[
                pl.ds(pl.multiple_of(k * WIDTH, WIDTH), WIDTH)
            ].reshape(8, SEQ)

        for k in range(full * 8, -(-vocab // SEQ)):
            count = min(SEQ, vocab - k * SEQ)
            table[k:k + 1, :count] = flat[pl.ds(k * SEQ, count)].reshape(1, count)
        ids = ids_ref[...]
        chosen = lax.broadcasted_iota(jnp.int32, (SEQ, SEQ), 0) == (ids & (SEQ - 1))
        columns = jnp.dot(
            table[...], jnp.where(chosen, 1.0, 0.0).astype(BF16), preferred_element_type=F32
        )
        row_hit = lax.broadcasted_iota(jnp.int32, columns.shape, 0) == (ids >> 7)
        found = jnp.sum(jnp.where(row_hit, columns, 0.0), axis=0, keepdims=True)
        own = jnp.where(lane < length_ref[0], found, 0.0)
        own = own / jnp.sum(own, axis=1, keepdims=True)
        tokw[OWN, 0] = jnp.broadcast_to(own, (8, SEQ))
        for k, (blk, s) in enumerate(USED):
            dy, flip_z = PLACES[blk]
            remote(
                tokw.at[OWN, 0], tokw.at[blk, s], tokw_send.at[k], tokw_sem.at[blk, s], device(-dy, flip_z, s)
            ).start()

    @pl.loop(0, SLOTS + 1)
    def _(k):
        @pl.when(k < SLOTS)
        def _():
            for s in range(PIECES):
                rows = rows_of(z, s)
                landed(wt.at[k, rows], slice_sem.at[k, s])

                @pl.when(k + 1 < SLOTS)
                def _(rows=rows, s=s):
                    remote(
                        wt.at[k, rows], wt.at[k + 1, rows], chain_send.at[k, s], slice_sem.at[k + 1, s], ahead
                    ).start()

                remote(wt.at[k, rows], wt.at[k, rows], z_send.at[k, s], z_sem.at[k, s], inner).start()

        @pl.when(k == 2)
        def _():
            landed(ctx.at[1], ctx_sem)

        @pl.when(k == 3)
        def _():
            token_weights()

        @pl.when((k == 2) | (k == 4))
        def _():
            for n in (0, 1):
                for s in range(PIECES):
                    landed(wt.at[k - 2 + n, rows_of(1 - z, s)], z_sem.at[k - 2 + n, s])
            both = lax.dot_general(
                ctx[...].reshape(2 * SEQ, WIDTH), wt[pl.ds(k - 2, 2)].reshape(2 * SEQ, WIDTH), NT,
                preferred_element_type=F32,
            )
            for n in (0, 1):
                at = columns_at(k - 2 + n, c)
                side = slice(n * SEQ, (n + 1) * SEQ)
                part[k - 2 + n] = both[SEQ:, side]
                remote(
                    part.at[k - 2 + n], mixed.at[:, at], part_send.at[k - 2 + n], part_sem.at[k - 2 + n], mate
                ).start()
                mixed[:, at] = both[:SEQ, side]

    for load in loads[4:]:
        load.wait()
    for k in range(SLOTS):
        landed(mixed.at[:, columns_at(k, 1 - c)], part_sem.at[k])

    def slot(blk, s, q):
        return units.at[blk, s, pl.ds(pl.multiple_of(q * ROWS, ROWS), ROWS)]

    moves = []

    def pass_on(src, dst, q, target):
        if (src, dst) not in moves:
            moves.append((src, dst))
        remote(
            slot(*src, q), slot(*dst, q), unit_send.at[moves.index((src, dst)), q],
            unit_sem.at[dst[0], dst[1], q], target,
        ).start()

    @pl.loop(0, CHUNKS)
    def _(q):
        rows = pl.ds(pl.multiple_of(q * ROWS, ROWS), ROWS)
        x = hid[rows, :].astype(F32) + mixed[rows, :] + params[0]
        centre = x - jnp.mean(x, axis=-1, keepdims=True)
        spread = jnp.mean(centre * centre, axis=-1, keepdims=True)
        embedded = (centre * lax.rsqrt(spread + 1e-07) * params[1] + params[2]).astype(BF16)
        embedded_out[0, rows, :] = embedded
        values = embedded.astype(F32)
        unit = values * lax.rsqrt(jnp.sum(values * values, axis=-1, keepdims=True) + 1e-06)

        @pl.when(q == 0)
        def _():
            first_unit[...] = unit[:1]

        real = lax.broadcasted_iota(jnp.int32, (ROWS, 1), 0) + q * ROWS < length_ref[0]
        units[OWN, 0, rows] = jnp.where(real, unit, first_unit[...]).astype(BF16)
        pass_on((OWN, 0), (M1, 0), q, up)
        pass_on((OWN, 0), (P1, 0), q, down)
        pass_on((OWN, 0), (OWN, 1), q, mate)

    def all_landed(blk, s):
        for q in range(CHUNKS):
            landed(slot(blk, s, q), unit_sem.at[blk, s, q])

    eye = lax.broadcasted_iota(jnp.int32, (SEQ, SEQ), 0) == lax.broadcasted_iota(jnp.int32, (SEQ, SEQ), 1)
    line = lax.broadcasted_iota(jnp.int32, (8, SEQ), 0)

    def two_lines(first, second):
        return jnp.where(line == 0, first, jnp.where(line == 1, second, 0.0))

    def score(sim, a, b, to_a=True):
        best_a = jnp.sum(jnp.where(eye, jnp.max(sim, axis=1, keepdims=True), 0.0), axis=0, keepdims=True)
        best_b = jnp.max(sim, axis=0, keepdims=True)
        p = jnp.sum(tokw[a[0], a[1], 0:1] * best_a, axis=1, keepdims=True)
        r = jnp.sum(tokw[b[0], b[1], 0:1] * best_b, axis=1, keepdims=True)
        lane_b = number(*b) if to_a is True else jnp.where(to_a, number(*b), -1)
        lane_a = number(*a)
        result[a[0], a[1]] = result[a[0], a[1]] + jnp.where(lane == lane_b, two_lines(p, r), 0.0)
        result[b[0], b[1]] = result[b[0], b[1]] + jnp.where(lane == lane_a, two_lines(r, p), 0.0)

    def single(blk, s, other):
        score(
            lax.dot_general(units[blk, s], units[other, 0], NT, preferred_element_type=F32), (blk, s), (other, 0)
        )

    def double(blk, s, other, keep_self=True):
        sims = lax.dot_general(
            units[blk, s], units[pl.ds(other, 2), 0].reshape(2 * SEQ, WIDTH), NT, preferred_element_type=F32
        )
        score(sims[:, :SEQ], (blk, s), (other, 0), keep_self)
        score(sims[:, SEQ:], (blk, s), (other + 1, 0))

    @pl.loop(0, 2 * CHUNKS)
    def _(t):
        @pl.when(t < CHUNKS)
        def _():
            q = t
            landed(slot(M1, 0, q), unit_sem.at[M1, 0, q])
            pass_on((M1, 0), (M2, 0), q, up)
            landed(slot(P1, 0, q), unit_sem.at[P1, 0, q])
            pass_on((P1, 0), (P2, 0), q, down)
            pass_on((P1, 0), (C1, 0), q, inner)
            pass_on((M1, 0), (M1, 1), q, mate)
            pass_on((P1, 0), (P1, 1), q, mate)

        @pl.when(t >= CHUNKS)
        def _():
            q = t - CHUNKS
            landed(slot(P2, 0, q), unit_sem.at[P2, 0, q])
            pass_on((P2, 0), (C2, 0), q, inner)
            landed(slot(M2, 0, q), unit_sem.at[M2, 0, q])
            pass_on((M2, 0), (M2, 1), q, mate)

        @pl.when(t == 2)
        def _():
            for blk, s in USED:
                landed(tokw.at[blk, s], tokw_sem.at[blk, s])

        for when, blk, s in ((4, OWN, 1), (5, C1, 0), (6, M1, 1)):
            @pl.when(t == when)
            def _(blk=blk, s=s):
                all_landed(blk, s)

        @pl.when(t >= 3)
        def _():
            left = jnp.where(t <= 4, OWN, jnp.where(t <= 6, M1, M2))
            sample = jnp.where((t == 4) | (t == 6), 1, 0)
            double(left, sample, jnp.where(t <= 4, OWN, P1), t >= 5)

    all_landed(P1, 1)

    @pl.loop(0, 3)
    def _(t):
        single(jnp.where(t < 2, OWN, P1), jnp.where(t < 2, t, z), C1)

    all_landed(M2, 1)
    double(M2, 1, P1)

    @pl.loop(0, 2)
    def _(t):
        @pl.when(t == 1)
        def _():
            all_landed(C2, 0)

        single(M2, jnp.where(t == 0, y // 4, z), P2 + t)

    for k, (blk, s) in enumerate(USED):
        dy, flip_z = PLACES[blk]
        remote(
            result.at[blk, s], arrived.at[k], result_send.at[k], result_sem.at[k], device(dy, flip_z, s)
        ).start()
    for k in range(len(USED)):
        landed(arrived.at[k], result_sem.at[k])
    everything = result[OWN, 0]
    for k in range(len(USED)):
        everything = everything + arrived[k]
    precision = everything[0:1]
    recall = everything[1:2]
    f_score = 2.0 * precision * recall / jnp.maximum(precision + recall, 0.25)
    others = jnp.where((lane < 32) & (lane != number(OWN, 0)), f_score, 0.0)
    utility = jnp.sum(others, axis=1, keepdims=True) / 31.0
    scores_out[...] = jnp.where(line < 2, everything, jnp.where(line == 2, f_score, utility))

    @pl.loop(0, CHUNKS)
    def _(q):
        for m, (src, _) in enumerate(moves):
            sent(slot(*src, q), unit_send.at[m, q])

    for k in range(SLOTS):
        for s in range(PIECES):
            piece = wt.at[k, rows_of(z, s)]
            if k + 1 < SLOTS:
                sent(piece, chain_send.at[k, s])
            sent(piece, z_send.at[k, s])
        sent(part.at[k], part_send.at[k])
    sent(ctx.at[0], ctx_send)
    for k, (blk, s) in enumerate(USED):
        sent(tokw.at[OWN, 0], tokw_send.at[k])
        sent(result.at[blk, s], result_send.at[k])
    for h in (0, 1):
        sent(own_piece(h)[0], first_sem.at[1, h])

    @pl.when(c == 1)
    def _():
        for h in (0, 1):
            sent(own_piece(h)[0], first_sem.at[0, h])


def hand_out(embedded_ref, scores_ref, embedded_hbm, precision_ref, recall_ref, f_ref, utility_ref, sem):
    copy = pltpu.make_async_copy(embedded_ref, embedded_hbm, sem)
    copy.start()
    precision_ref[...] = scores_ref[0:1, :32]
    recall_ref[...] = scores_ref[1:2, :32]
    f_ref[...] = scores_ref[2:3, :32]
    utility_ref[...] = scores_ref[3:4, :1]
    copy.wait()


def local(
    context, hidden, out_weight, out_bias, norm_gain, norm_bias, token_ids, lengths, idf_table
):
    vocab = idf_table.shape[0]
    table_rows = vocab // WIDTH * 8 + 16
    vmem = pl.BlockSpec(memory_space=pltpu.VMEM)
    hbm = pl.BlockSpec(memory_space=pl.ANY)
    dma = pltpu.SemaphoreType.DMA
    count = len(USED)
    embedded, scores = pl.pallas_call(
        kernel,
        out_shape=(
            jax.ShapeDtypeStruct((1, SEQ, WIDTH), BF16),
            jax.ShapeDtypeStruct((8, SEQ), F32),
        ),
        in_specs=[hbm] * 9,
        out_specs=(vmem, vmem),
        scratch_shapes=[
            pltpu.VMEM((2, SEQ, WIDTH), BF16),
            pltpu.VMEM((SEQ, WIDTH), BF16),
            pltpu.VMEM((SLOTS, SEQ, WIDTH), BF16),
            pltpu.VMEM((SLOTS, SEQ, SEQ), F32),
            pltpu.VMEM((SEQ, WIDTH), F32),
            pltpu.VMEM((3, 1, WIDTH), F32),
            pltpu.VMEM((1, SEQ), jnp.int32),
            pltpu.SMEM((1,), jnp.int32),
            pltpu.VMEM((vocab,), BF16),
            pltpu.VMEM((table_rows, SEQ), BF16),
            pltpu.VMEM((7, 2, SEQ, WIDTH), BF16),
            pltpu.VMEM((1, WIDTH), F32),
            pltpu.VMEM((7, 2, 8, SEQ), F32),
            pltpu.VMEM((7, 2, 8, SEQ), F32),
            pltpu.VMEM((count, 8, SEQ), F32),
            dma((8,)),
            dma((2, 2)),
            dma((SLOTS - 1, PIECES)),
            dma((SLOTS, PIECES)),
            dma,
            dma((SLOTS,)),
            dma((count,)),
            dma((10, CHUNKS)),
            dma((count,)),
            dma((SLOTS, PIECES)),
            dma((SLOTS, PIECES)),
            dma,
            dma((SLOTS,)),
            dma((7, 2)),
            dma((7, 2, CHUNKS)),
            dma((count,)),
        ],
        compiler_params=pltpu.CompilerParams(
            collective_id=0, has_side_effects=True, vmem_limit_bytes=60 * 1024 * 1024
        ),
        cost_estimate=pl.CostEstimate(flops=1 << 30, bytes_accessed=1 << 20, transcendentals=0),
    )(
        context, hidden, out_weight.T, out_bias.reshape(1, WIDTH), norm_gain.reshape(1, WIDTH),
        norm_bias.reshape(1, WIDTH), token_ids, lengths, idf_table,
    )
    embedded, precision, recall, f_score, utility = pl.pallas_call(
        hand_out,
        out_shape=(
            jax.ShapeDtypeStruct((1, SEQ, WIDTH), BF16),
            jax.ShapeDtypeStruct((1, 32), F32),
            jax.ShapeDtypeStruct((1, 32), F32),
            jax.ShapeDtypeStruct((1, 32), F32),
            jax.ShapeDtypeStruct((1, 1), F32),
        ),
        in_specs=[vmem, vmem],
        out_specs=(pl.BlockSpec(memory_space=pl.ANY), vmem, vmem, vmem, vmem),
        scratch_shapes=[dma],
    )(embedded, scores)
    return embedded, precision, recall, f_score, utility.reshape(1)


def solution(mesh):
    placed = (
        P(("doc", "samp", "tok"), None, None),
        P(("doc", "samp", "tok"), None, None),
        P(None, ("samp", "tok")),
        P(),
        P(),
        P(),
        P(("doc", "samp", "tok"), None),
        P(("doc", "samp", "tok")),
        P(),
    )
    return jax.shard_map(
        local,
        mesh=mesh,
        in_specs=placed,
        out_specs=(
            P(("doc", "samp", "tok"), None, None),
            P(("doc", "samp", "tok"), None),
            P(("doc", "samp", "tok"), None),
            P(("doc", "samp", "tok"), None),
            P(("doc", "samp", "tok")),
        ),
        check_vma=False,
    )
```

```python
import jax
import jax.numpy as jnp
from jax import lax
from jax.experimental import pallas as pl
from jax.experimental.pallas import tpu as pltpu
from jax.sharding import PartitionSpec as P

MESH = pl.DeviceIdType.MESH
F32 = jnp.float32
BF16 = jnp.bfloat16

SEQ = 128
WIDTH = 1024
RING = 8
SLICE = 32
SLOTS = 4
PIECE = 16
PIECES = 2 * SLICE // PIECE
CHUNKS = 4
ROWS = SEQ // CHUNKS
NT = (((1,), (1,)), ((), ()))

OWN, M1, M2, P1, C1, P2, C2 = range(7)
PLACES = {OWN: (0, 0), M1: (-1, 0), M2: (-2, 0), P1: (1, 0), C1: (1, 1), P2: (2, 0), C2: (2, 1)}
USED = [(OWN, 1), (M1, 0), (M1, 1), (M2, 0), (M2, 1), (P1, 0), (P1, 1), (C1, 0), (P2, 0), (C2, 0)]


def kernel(
    context_hbm, hidden_hbm, weight_hbm, bias_hbm, gain_hbm, shift_hbm, ids_hbm, length_hbm, table_hbm,
    embedded_out, scores_out,
    ctx, hid, wt, part, mixed, params, ids_ref, length_ref, flat, table, units, first_unit, tokw, result, arrived,
    load_sem, first_sem, chain_send, z_send, side_send, ctx_send, part_send, tokw_send, unit_send, result_send,
    slice_sem, z_sem, ctx_sem, part_sem, tokw_sem, unit_sem, result_sem,
):
    doc = lax.axis_index("doc")
    y = lax.axis_index("samp")
    tok = lax.axis_index("tok")
    z, c = tok // 2, tok % 2

    def device(dy, flip_z, flip_c):
        yy = (y + dy + RING) % RING
        zz = 1 - z if flip_z else z
        cc = 1 - c if flip_c else c
        return (doc, yy, zz * 2 + cc)

    def number(blk, s):
        dy = jnp.where(blk <= M2, -blk, (blk - 1) // 2)
        flip = jnp.where((blk == C1) | (blk == C2), 1, 0)
        return (y + dy + RING) % RING * 4 + (z + flip) % 2 * 2 + (c + s) % 2

    up, down, inner, mate = device(1, 0, 0), device(-1, 0, 0), device(0, 1, 0), device(0, 0, 1)
    ahead = device(1 - 2 * c, 0, 0)

    def rows_of(zz, piece):
        return pl.ds(pl.multiple_of(zz * 2 * SLICE + piece * PIECE, PIECE), PIECE)

    def own_piece(h):
        return weight_hbm.at[pl.ds(h * PIECE, PIECE)], wt.at[0, rows_of(z, c * 2 + h)]

    @pl.when(c == 0)
    def _():
        for h in (0, 1):
            pltpu.make_async_copy(*own_piece(h), slice_sem.at[0, h]).start()

    loads = [
        pltpu.make_async_copy(context_hbm.at[0], ctx.at[0], load_sem.at[0]),
        pltpu.make_async_copy(table_hbm, flat, load_sem.at[1]),
        pltpu.make_async_copy(ids_hbm, ids_ref, load_sem.at[2]),
        pltpu.make_async_copy(length_hbm, length_ref, load_sem.at[3]),
        pltpu.make_async_copy(hidden_hbm.at[0], hid, load_sem.at[4]),
        pltpu.make_async_copy(bias_hbm, params.at[0], load_sem.at[5]),
        pltpu.make_async_copy(gain_hbm, params.at[1], load_sem.at[6]),
        pltpu.make_async_copy(shift_hbm, params.at[2], load_sem.at[7]),
    ]
    for load in loads:
        load.start()

    partners = [inner, mate]
    partners += [device(dy, 0, fc) for dy in (1, -1, 2, -2) for fc in (0, 1)]
    partners += [device(dy, 1, 0) for dy in (1, -1, 2, -2)]
    barrier = pltpu.get_barrier_semaphore()
    for partner in partners:
        pl.semaphore_signal(barrier, inc=1, device_id=partner, device_id_type=MESH)

    def remote(src, dst, send_sem, recv_sem, target):
        return pltpu.make_async_remote_copy(
            src_ref=src, dst_ref=dst, send_sem=send_sem, recv_sem=recv_sem,
            device_id=target, device_id_type=MESH,
        )

    def landed(dst, recv_sem):
        remote(dst, dst, ctx_send, recv_sem, mate).wait_recv()

    def sent(src, send_sem):
        remote(src, src, send_sem, ctx_sem, mate).wait_send()

    result[...] = jnp.zeros_like(result)
    pl.semaphore_wait(barrier, len(partners))

    below = (doc, (y + RING - 1) % RING, z * 2 + 1)

    for h in (0, 1):
        @pl.when(c == 0)
        def _(h=h):
            remote(*own_piece(h), first_sem.at[1, h], slice_sem.at[0, h], below).start()

        @pl.when(c == 1)
        def _(h=h):
            remote(*own_piece(h), first_sem.at[1, h], slice_sem.at[0, 2 + h], below).start()
            remote(*own_piece(h), first_sem.at[0, h], slice_sem.at[0, 2 + h], mate).start()

    loads[0].wait()
    remote(ctx.at[0], ctx.at[1], ctx_send, ctx_sem, mate).start()

    def columns_at(k, core):
        yy = (y + RING + jnp.where(core == 0, -k, k + 1)) % RING
        return pl.ds(pl.multiple_of(yy * SEQ, SEQ), SEQ)

    lane = lax.broadcasted_iota(jnp.int32, (1, SEQ), 1)

    def token_weights():
        for load in loads[1:4]:
            load.wait()
        vocab = flat.shape[0]
        full = vocab // WIDTH
        table[pl.ds(full * 8, 16)] = jnp.zeros((16, SEQ), BF16)

        @pl.loop(0, full)
        def _(k):
            table[pl.ds(pl.multiple_of(k * 8, 8), 8)] = flat[
                pl.ds(pl.multiple_of(k * WIDTH, WIDTH), WIDTH)
            ].reshape(8, SEQ)

        for k in range(full * 8, -(-vocab // SEQ)):
            count = min(SEQ, vocab - k * SEQ)
            table[k:k + 1, :count] = flat[pl.ds(k * SEQ, count)].reshape(1, count)
        ids = ids_ref[...]
        chosen = lax.broadcasted_iota(jnp.int32, (SEQ, SEQ), 0) == (ids & (SEQ - 1))
        columns = jnp.dot(
            table[...], jnp.where(chosen, 1.0, 0.0).astype(BF16), preferred_element_type=F32
        )
        row_hit = lax.broadcasted_iota(jnp.int32, columns.shape, 0) == (ids >> 7)
        found = jnp.sum(jnp.where(row_hit, columns, 0.0), axis=0, keepdims=True)
        own = jnp.where(lane < length_ref[0], found, 0.0)
        own = own / jnp.sum(own, axis=1, keepdims=True)
        tokw[OWN, 0] = jnp.broadcast_to(own, (8, SEQ))
        for k, (blk, s) in enumerate(USED):
            dy, flip_z = PLACES[blk]
            remote(
                tokw.at[OWN, 0], tokw.at[blk, s], tokw_send.at[k], tokw_sem.at[blk, s], device(-dy, flip_z, s)
            ).start()

    @pl.loop(0, SLOTS + 1)
    def _(k):
        @pl.when(k < SLOTS)
        def _():
            for s in range(PIECES):
                rows = rows_of(z, s)
                landed(wt.at[k, rows], slice_sem.at[k, s])

                @pl.when(k + 1 < SLOTS)
                def _(rows=rows, s=s):
                    remote(
                        wt.at[k, rows], wt.at[k + 1, rows], chain_send.at[k, s], slice_sem.at[k + 1, s], ahead
                    ).start()

                @pl.when((k == 0) | (s < PIECES // 2))
                def _(rows=rows, s=s):
                    remote(wt.at[k, rows], wt.at[k, rows], z_send.at[k, s], z_sem.at[k, s], inner).start()

        @pl.when(k >= 1)
        def _():
            for s in range(PIECES // 2, PIECES):
                rows = rows_of(1 - z, s)
                landed(wt.at[k - 1, rows], z_sem.at[k - 1, s])

                @pl.when(k < SLOTS)
                def _(rows=rows, s=s):
                    remote(
                        wt.at[k - 1, rows], wt.at[k, rows], side_send.at[k - 1, s - PIECES // 2], z_sem.at[k, s], ahead
                    ).start()

        @pl.when(k == 3)
        def _():
            landed(ctx.at[1], ctx_sem)

        @pl.when(k >= 3)
        def _():
            first = (k - 3) * 2
            for n in (0, 1):
                for s in range(PIECES // 2):
                    landed(wt.at[first + n, rows_of(1 - z, s)], z_sem.at[first + n, s])
            both = lax.dot_general(
                ctx[...].reshape(2 * SEQ, WIDTH), wt[pl.ds(first, 2)].reshape(2 * SEQ, WIDTH), NT,
                preferred_element_type=F32,
            )
            for n in (0, 1):
                at = columns_at(first + n, c)
                side = slice(n * SEQ, (n + 1) * SEQ)
                part[first + n] = both[SEQ:, side]
                remote(
                    part.at[first + n], mixed.at[:, at], part_send.at[first + n], part_sem.at[first + n], mate
                ).start()
                mixed[:, at] = both[:SEQ, side]

        @pl.when(k == 3)
        def _():
            token_weights()

    for load in loads[4:]:
        load.wait()
    for k in range(SLOTS):
        landed(mixed.at[:, columns_at(k, 1 - c)], part_sem.at[k])

    def slot(blk, s, q):
        return units.at[blk, s, pl.ds(pl.multiple_of(q * ROWS, ROWS), ROWS)]

    moves = []

    def pass_on(src, dst, q, target):
        if (src, dst) not in moves:
            moves.append((src, dst))
        remote(
            slot(*src, q), slot(*dst, q), unit_send.at[moves.index((src, dst)), q],
            unit_sem.at[dst[0], dst[1], q], target,
        ).start()

    @pl.loop(0, CHUNKS)
    def _(q):
        rows = pl.ds(pl.multiple_of(q * ROWS, ROWS), ROWS)
        x = hid[rows, :].astype(F32) + mixed[rows, :] + params[0]
        centre = x - jnp.mean(x, axis=-1, keepdims=True)
        spread = jnp.mean(centre * centre, axis=-1, keepdims=True)
        embedded = (centre * lax.rsqrt(spread + 1e-07) * params[1] + params[2]).astype(BF16)
        embedded_out[0, rows, :] = embedded
        values = embedded.astype(F32)
        unit = values * lax.rsqrt(jnp.sum(values * values, axis=-1, keepdims=True) + 1e-06)

        @pl.when(q == 0)
        def _():
            first_unit[...] = unit[:1]

        real = lax.broadcasted_iota(jnp.int32, (ROWS, 1), 0) + q * ROWS < length_ref[0]
        units[OWN, 0, rows] = jnp.where(real, unit, first_unit[...]).astype(BF16)
        pass_on((OWN, 0), (M1, 0), q, up)
        pass_on((OWN, 0), (P1, 0), q, down)
        pass_on((OWN, 0), (OWN, 1), q, mate)

    for k in range(SLOTS):
        for s in range(PIECES):
            if k + 1 < SLOTS:
                sent(wt.at[k, rows_of(z, s)], chain_send.at[k, s])
                if s >= PIECES // 2:
                    sent(wt.at[k, rows_of(1 - z, s)], side_send.at[k, s - PIECES // 2])
            if k == 0 or s < PIECES // 2:
                sent(wt.at[k, rows_of(z, s)], z_send.at[k, s])
        sent(part.at[k], part_send.at[k])
    sent(ctx.at[0], ctx_send)
    for k in range(len(USED)):
        sent(tokw.at[OWN, 0], tokw_send.at[k])
    for h in (0, 1):
        sent(own_piece(h)[0], first_sem.at[1, h])

    @pl.when(c == 1)
    def _():
        for h in (0, 1):
            sent(own_piece(h)[0], first_sem.at[0, h])

    def all_landed(blk, s):
        for q in range(CHUNKS):
            landed(slot(blk, s, q), unit_sem.at[blk, s, q])

    eye = lax.broadcasted_iota(jnp.int32, (SEQ, SEQ), 0) == lax.broadcasted_iota(jnp.int32, (SEQ, SEQ), 1)
    line = lax.broadcasted_iota(jnp.int32, (8, SEQ), 0)

    def two_lines(first, second):
        return jnp.where(line == 0, first, jnp.where(line == 1, second, 0.0))

    def score(sim, a, b, to_a=True):
        best_a = jnp.sum(jnp.where(eye, jnp.max(sim, axis=1, keepdims=True), 0.0), axis=0, keepdims=True)
        best_b = jnp.max(sim, axis=0, keepdims=True)
        p = jnp.sum(tokw[a[0], a[1], 0:1] * best_a, axis=1, keepdims=True)
        r = jnp.sum(tokw[b[0], b[1], 0:1] * best_b, axis=1, keepdims=True)
        lane_b = number(*b) if to_a is True else jnp.where(to_a, number(*b), -1)
        lane_a = number(*a)
        result[a[0], a[1]] = result[a[0], a[1]] + jnp.where(lane == lane_b, two_lines(p, r), 0.0)
        result[b[0], b[1]] = result[b[0], b[1]] + jnp.where(lane == lane_a, two_lines(r, p), 0.0)

    def single(blk, s, other):
        score(
            lax.dot_general(units[blk, s], units[other, 0], NT, preferred_element_type=F32), (blk, s), (other, 0)
        )

    def double(blk, s, other, keep_self=True):
        sims = lax.dot_general(
            units[blk, s], units[pl.ds(other, 2), 0].reshape(2 * SEQ, WIDTH), NT, preferred_element_type=F32
        )
        score(sims[:, :SEQ], (blk, s), (other, 0), keep_self)
        score(sims[:, SEQ:], (blk, s), (other + 1, 0))

    @pl.loop(0, 2 * CHUNKS)
    def _(t):
        @pl.when(t < CHUNKS)
        def _():
            q = t
            landed(slot(M1, 0, q), unit_sem.at[M1, 0, q])
            pass_on((M1, 0), (M2, 0), q, up)
            landed(slot(P1, 0, q), unit_sem.at[P1, 0, q])
            pass_on((P1, 0), (P2, 0), q, down)
            pass_on((P1, 0), (C1, 0), q, inner)
            pass_on((M1, 0), (M1, 1), q, mate)
            pass_on((P1, 0), (P1, 1), q, mate)

        @pl.when(t >= CHUNKS)
        def _():
            q = t - CHUNKS
            landed(slot(P2, 0, q), unit_sem.at[P2, 0, q])
            pass_on((P2, 0), (C2, 0), q, inner)
            landed(slot(M2, 0, q), unit_sem.at[M2, 0, q])
            pass_on((M2, 0), (M2, 1), q, mate)

        @pl.when(t == 2)
        def _():
            for blk, s in USED:
                landed(tokw.at[blk, s], tokw_sem.at[blk, s])

        for when, blk, s in ((4, OWN, 1), (5, C1, 0), (6, M1, 1)):
            @pl.when(t == when)
            def _(blk=blk, s=s):
                all_landed(blk, s)

        @pl.when(t >= 3)
        def _():
            left = jnp.where(t <= 4, OWN, jnp.where(t <= 6, M1, M2))
            sample = jnp.where((t == 4) | (t == 6), 1, 0)
            double(left, sample, jnp.where(t <= 4, OWN, P1), t >= 5)

    all_landed(P1, 1)

    @pl.loop(0, 3)
    def _(t):
        single(jnp.where(t < 2, OWN, P1), jnp.where(t < 2, t, z), C1)

    all_landed(M2, 1)
    double(M2, 1, P1)

    @pl.loop(0, 2)
    def _(t):
        @pl.when(t == 1)
        def _():
            all_landed(C2, 0)

        single(M2, jnp.where(t == 0, y // 4, z), P2 + t)

    for k, (blk, s) in enumerate(USED):
        dy, flip_z = PLACES[blk]
        remote(
            result.at[blk, s], arrived.at[k], result_send.at[k], result_sem.at[k], device(dy, flip_z, s)
        ).start()
    @pl.loop(0, CHUNKS)
    def _(q):
        for m, (src, _) in enumerate(moves):
            sent(slot(*src, q), unit_send.at[m, q])

    for k, (blk, s) in enumerate(USED):
        sent(result.at[blk, s], result_send.at[k])
    for k in range(len(USED)):
        landed(arrived.at[k], result_sem.at[k])
    everything = result[OWN, 0]
    for k in range(len(USED)):
        everything = everything + arrived[k]
    precision = everything[0:1]
    recall = everything[1:2]
    f_score = 2.0 * precision * recall / jnp.maximum(precision + recall, 0.25)
    others = jnp.where((lane < 32) & (lane != number(OWN, 0)), f_score, 0.0)
    utility = jnp.sum(others, axis=1, keepdims=True) / 31.0
    scores_out[...] = jnp.where(line < 2, everything, jnp.where(line == 2, f_score, utility))


def hand_out(embedded_ref, scores_ref, embedded_hbm, precision_ref, recall_ref, f_ref, utility_ref, sem):
    copy = pltpu.make_async_copy(embedded_ref, embedded_hbm, sem)
    copy.start()
    precision_ref[...] = scores_ref[0:1, :32]
    recall_ref[...] = scores_ref[1:2, :32]
    f_ref[...] = scores_ref[2:3, :32]
    utility_ref[...] = scores_ref[3:4, :1]
    copy.wait()


def local(
    context, hidden, out_weight, out_bias, norm_gain, norm_bias, token_ids, lengths, idf_table
):
    vocab = idf_table.shape[0]
    table_rows = vocab // WIDTH * 8 + 16
    vmem = pl.BlockSpec(memory_space=pltpu.VMEM)
    hbm = pl.BlockSpec(memory_space=pl.ANY)
    dma = pltpu.SemaphoreType.DMA
    count = len(USED)
    embedded, scores = pl.pallas_call(
        kernel,
        out_shape=(
            jax.ShapeDtypeStruct((1, SEQ, WIDTH), BF16),
            jax.ShapeDtypeStruct((8, SEQ), F32),
        ),
        in_specs=[hbm] * 9,
        out_specs=(vmem, vmem),
        scratch_shapes=[
            pltpu.VMEM((2, SEQ, WIDTH), BF16),
            pltpu.VMEM((SEQ, WIDTH), BF16),
            pltpu.VMEM((SLOTS, SEQ, WIDTH), BF16),
            pltpu.VMEM((SLOTS, SEQ, SEQ), F32),
            pltpu.VMEM((SEQ, WIDTH), F32),
            pltpu.VMEM((3, 1, WIDTH), F32),
            pltpu.VMEM((1, SEQ), jnp.int32),
            pltpu.SMEM((1,), jnp.int32),
            pltpu.VMEM((vocab,), BF16),
            pltpu.VMEM((table_rows, SEQ), BF16),
            pltpu.VMEM((7, 2, SEQ, WIDTH), BF16),
            pltpu.VMEM((1, WIDTH), F32),
            pltpu.VMEM((7, 2, 8, SEQ), F32),
            pltpu.VMEM((7, 2, 8, SEQ), F32),
            pltpu.VMEM((count, 8, SEQ), F32),
            dma((8,)),
            dma((2, 2)),
            dma((SLOTS - 1, PIECES)),
            dma((SLOTS, PIECES)),
            dma((SLOTS - 1, PIECES // 2)),
            dma,
            dma((SLOTS,)),
            dma((count,)),
            dma((10, CHUNKS)),
            dma((count,)),
            dma((SLOTS, PIECES)),
            dma((SLOTS, PIECES)),
            dma,
            dma((SLOTS,)),
            dma((7, 2)),
            dma((7, 2, CHUNKS)),
            dma((count,)),
        ],
        compiler_params=pltpu.CompilerParams(
            collective_id=0, has_side_effects=True, vmem_limit_bytes=60 * 1024 * 1024
        ),
        cost_estimate=pl.CostEstimate(flops=1 << 30, bytes_accessed=1 << 20, transcendentals=0),
    )(
        context, hidden, out_weight.T, out_bias.reshape(1, WIDTH), norm_gain.reshape(1, WIDTH),
        norm_bias.reshape(1, WIDTH), token_ids, lengths, idf_table,
    )
    embedded, precision, recall, f_score, utility = pl.pallas_call(
        hand_out,
        out_shape=(
            jax.ShapeDtypeStruct((1, SEQ, WIDTH), BF16),
            jax.ShapeDtypeStruct((1, 32), F32),
            jax.ShapeDtypeStruct((1, 32), F32),
            jax.ShapeDtypeStruct((1, 32), F32),
            jax.ShapeDtypeStruct((1, 1), F32),
        ),
        in_specs=[vmem, vmem],
        out_specs=(pl.BlockSpec(memory_space=pl.ANY), vmem, vmem, vmem, vmem),
        scratch_shapes=[dma],
    )(embedded, scores)
    return embedded, precision, recall, f_score, utility.reshape(1)


def solution(mesh):
    placed = (
        P(("doc", "samp", "tok"), None, None),
        P(("doc", "samp", "tok"), None, None),
        P(None, ("samp", "tok")),
        P(),
        P(),
        P(),
        P(("doc", "samp", "tok"), None),
        P(("doc", "samp", "tok")),
        P(),
    )
    return jax.shard_map(
        local,
        mesh=mesh,
        in_specs=placed,
        out_specs=(
            P(("doc", "samp", "tok"), None, None),
            P(("doc", "samp", "tok"), None),
            P(("doc", "samp", "tok"), None),
            P(("doc", "samp", "tok"), None),
            P(("doc", "samp", "tok")),
        ),
        check_vma=False,
    )
```

```python
import jax
import jax.numpy as jnp
from jax import lax
from jax.experimental import pallas as pl
from jax.experimental.pallas import tpu as pltpu
from jax.sharding import PartitionSpec as P

MESH = pl.DeviceIdType.MESH
F32 = jnp.float32
BF16 = jnp.bfloat16

SEQ = 128
WIDTH = 1024
RING = 8
SLICE = 32
SLOTS = 4
PIECE = 16
PIECES = 2 * SLICE // PIECE
CHUNKS = 4
ROWS = SEQ // CHUNKS
NT = (((1,), (1,)), ((), ()))

OWN, M1, M2, P1, C1, P2, C2 = range(7)
PLACES = {OWN: (0, 0), M1: (-1, 0), M2: (-2, 0), P1: (1, 0), C1: (1, 1), P2: (2, 0), C2: (2, 1)}
USED = [(OWN, 1), (M1, 0), (M1, 1), (M2, 0), (M2, 1), (P1, 0), (C1, 0), (P2, 0), (C2, 0)]


def kernel(
    context_hbm, hidden_hbm, weight_hbm, bias_hbm, gain_hbm, shift_hbm, ids_hbm, length_hbm, table_hbm,
    embedded_out, scores_out,
    ctx, hid, wt, part, mixed, params, ids_ref, length_ref, flat, table, emb, units, first_unit, tokw, result, arrived,
    load_sem, store_sem, first_sem, chain_send, z_send, side_send, ctx_send, part_send, tokw_send, unit_send, result_send,
    slice_sem, z_sem, ctx_sem, part_sem, tokw_sem, unit_sem, result_sem,
):
    doc = lax.axis_index("doc")
    y = lax.axis_index("samp")
    tok = lax.axis_index("tok")
    z, c = tok // 2, tok % 2

    def device(dy, flip_z, flip_c):
        yy = (y + dy + RING) % RING
        zz = 1 - z if flip_z else z
        return (doc, yy, zz * 2 + (c + flip_c) % 2)

    def holder(blk, s):
        dy, flip_z = PLACES[blk]
        return device(-dy, flip_z, s + (1 - z if flip_z else 0))

    def owner(blk, s):
        dy, flip_z = PLACES[blk]
        return device(dy, flip_z, s + (z if flip_z else 0))

    def number(blk, s):
        dy = jnp.where(blk <= M2, -blk, (blk - 1) // 2)
        flip = jnp.where((blk == C1) | (blk == C2), 1, 0)
        return (y + dy + RING) % RING * 4 + (z + flip) % 2 * 2 + (c + s + flip * z) % 2

    up, down, inner, mate = device(1, 0, 0), device(-1, 0, 0), device(0, 1, 0), device(0, 0, 1)
    ahead = device(1 - 2 * c, 0, 0)
    across = device(0, 1, 1 - z)

    def rows_of(zz, piece):
        return pl.ds(pl.multiple_of(zz * 2 * SLICE + piece * PIECE, PIECE), PIECE)

    def own_piece(h):
        return weight_hbm.at[pl.ds(h * PIECE, PIECE)], wt.at[0, rows_of(z, c * 2 + h)]

    @pl.when(c == 0)
    def _():
        for h in (0, 1):
            pltpu.make_async_copy(*own_piece(h), slice_sem.at[0, h]).start()

    loads = [
        pltpu.make_async_copy(context_hbm.at[0], ctx.at[0], load_sem.at[0]),
        pltpu.make_async_copy(table_hbm, flat, load_sem.at[1]),
        pltpu.make_async_copy(ids_hbm, ids_ref, load_sem.at[2]),
        pltpu.make_async_copy(length_hbm, length_ref, load_sem.at[3]),
        pltpu.make_async_copy(hidden_hbm.at[0], hid, load_sem.at[4]),
        pltpu.make_async_copy(bias_hbm, params.at[0], load_sem.at[5]),
        pltpu.make_async_copy(gain_hbm, params.at[1], load_sem.at[6]),
        pltpu.make_async_copy(shift_hbm, params.at[2], load_sem.at[7]),
    ]
    for load in loads:
        load.start()

    partners = [inner, device(0, 1, 1), mate]
    partners += [device(dy, 0, fc) for dy in (1, -1, 2, -2) for fc in (0, 1)]
    partners += [device(dy, 1, z) for dy in (1, 2)]
    partners += [device(dy, 1, 1 - z) for dy in (-1, -2)]
    barrier = pltpu.get_barrier_semaphore()
    for partner in partners:
        pl.semaphore_signal(barrier, inc=1, device_id=partner, device_id_type=MESH)

    def remote(src, dst, send_sem, recv_sem, target):
        return pltpu.make_async_remote_copy(
            src_ref=src, dst_ref=dst, send_sem=send_sem, recv_sem=recv_sem,
            device_id=target, device_id_type=MESH,
        )

    def landed(dst, recv_sem):
        remote(dst, dst, ctx_send, recv_sem, mate).wait_recv()

    def sent(src, send_sem):
        remote(src, src, send_sem, ctx_sem, mate).wait_send()

    result[...] = jnp.zeros_like(result)
    pl.semaphore_wait(barrier, len(partners))

    below = (doc, (y + RING - 1) % RING, z * 2 + 1)

    for h in (0, 1):
        @pl.when(c == 0)
        def _(h=h):
            remote(*own_piece(h), first_sem.at[1, h], slice_sem.at[0, h], below).start()

        @pl.when(c == 1)
        def _(h=h):
            remote(*own_piece(h), first_sem.at[1, h], slice_sem.at[0, 2 + h], below).start()
            remote(*own_piece(h), first_sem.at[0, h], slice_sem.at[0, 2 + h], mate).start()

    loads[0].wait()
    remote(ctx.at[0], ctx.at[1], ctx_send, ctx_sem, mate).start()

    def columns_at(k, core):
        yy = (y + RING + jnp.where(core == 0, -k, k + 1)) % RING
        return pl.ds(pl.multiple_of(yy * SEQ, SEQ), SEQ)

    lane = lax.broadcasted_iota(jnp.int32, (1, SEQ), 1)

    def token_weights():
        for load in loads[1:4]:
            load.wait()
        vocab = flat.shape[0]
        full = vocab // WIDTH
        table[pl.ds(full * 8, 16)] = jnp.zeros((16, SEQ), BF16)

        @pl.loop(0, full)
        def _(k):
            table[pl.ds(pl.multiple_of(k * 8, 8), 8)] = flat[
                pl.ds(pl.multiple_of(k * WIDTH, WIDTH), WIDTH)
            ].reshape(8, SEQ)

        for k in range(full * 8, -(-vocab // SEQ)):
            count = min(SEQ, vocab - k * SEQ)
            table[k:k + 1, :count] = flat[pl.ds(k * SEQ, count)].reshape(1, count)
        ids = ids_ref[...]
        chosen = lax.broadcasted_iota(jnp.int32, (SEQ, SEQ), 0) == (ids & (SEQ - 1))
        columns = jnp.dot(
            table[...], jnp.where(chosen, 1.0, 0.0).astype(BF16), preferred_element_type=F32
        )
        row_hit = lax.broadcasted_iota(jnp.int32, columns.shape, 0) == (ids >> 7)
        found = jnp.sum(jnp.where(row_hit, columns, 0.0), axis=0, keepdims=True)
        own = jnp.where(lane < length_ref[0], found, 0.0)
        own = own / jnp.sum(own, axis=1, keepdims=True)
        tokw[OWN, 0] = jnp.broadcast_to(own, (8, SEQ))
        for k, (blk, s) in enumerate(USED):
            remote(
                tokw.at[OWN, 0], tokw.at[blk, s], tokw_send.at[k], tokw_sem.at[blk, s], holder(blk, s)
            ).start()

    @pl.loop(0, SLOTS + 1)
    def _(k):
        @pl.when(k < SLOTS)
        def _():
            for s in range(PIECES):
                rows = rows_of(z, s)
                landed(wt.at[k, rows], slice_sem.at[k, s])

                @pl.when(k + 1 < SLOTS)
                def _(rows=rows, s=s):
                    remote(
                        wt.at[k, rows], wt.at[k + 1, rows], chain_send.at[k, s], slice_sem.at[k + 1, s], ahead
                    ).start()

                @pl.when((k == 0) | (s < PIECES // 2))
                def _(rows=rows, s=s):
                    remote(wt.at[k, rows], wt.at[k, rows], z_send.at[k, s], z_sem.at[k, s], inner).start()

        @pl.when(k >= 1)
        def _():
            for s in range(PIECES // 2, PIECES):
                rows = rows_of(1 - z, s)
                landed(wt.at[k - 1, rows], z_sem.at[k - 1, s])

                @pl.when(k < SLOTS)
                def _(rows=rows, s=s):
                    remote(
                        wt.at[k - 1, rows], wt.at[k, rows], side_send.at[k - 1, s - PIECES // 2], z_sem.at[k, s], ahead
                    ).start()

        @pl.when(k == 3)
        def _():
            landed(ctx.at[1], ctx_sem)

        @pl.when(k >= 3)
        def _():
            first = (k - 3) * 2
            for n in (0, 1):
                for s in range(PIECES // 2):
                    landed(wt.at[first + n, rows_of(1 - z, s)], z_sem.at[first + n, s])
            both = lax.dot_general(
                ctx[...].reshape(2 * SEQ, WIDTH), wt[pl.ds(first, 2)].reshape(2 * SEQ, WIDTH), NT,
                preferred_element_type=F32,
            )
            for n in (0, 1):
                at = columns_at(first + n, c)
                side = slice(n * SEQ, (n + 1) * SEQ)
                part[first + n] = both[SEQ:, side]
                remote(
                    part.at[first + n], mixed.at[:, at], part_send.at[first + n], part_sem.at[first + n], mate
                ).start()
                mixed[:, at] = both[:SEQ, side]

        @pl.when(k == 3)
        def _():
            token_weights()

    for load in loads[4:]:
        load.wait()
    for k in range(SLOTS):
        landed(mixed.at[:, columns_at(k, 1 - c)], part_sem.at[k])

    def slot(blk, s, q):
        return units.at[blk, s, pl.ds(pl.multiple_of(q * ROWS, ROWS), ROWS)]

    moves = []

    def pass_on(src, dst, q, target):
        if (src, dst) not in moves:
            moves.append((src, dst))
        remote(
            slot(*src, q), slot(*dst, q), unit_send.at[moves.index((src, dst)), q],
            unit_sem.at[dst[0], dst[1], q], target,
        ).start()

    @pl.loop(0, CHUNKS)
    def _(q):
        rows = pl.ds(pl.multiple_of(q * ROWS, ROWS), ROWS)
        x = hid[rows, :].astype(F32) + mixed[rows, :] + params[0]
        centre = x - jnp.mean(x, axis=-1, keepdims=True)
        spread = jnp.mean(centre * centre, axis=-1, keepdims=True)
        embedded = (centre * lax.rsqrt(spread + 1e-07) * params[1] + params[2]).astype(BF16)
        emb[rows, :] = embedded
        values = embedded.astype(F32)
        unit = values * lax.rsqrt(jnp.sum(values * values, axis=-1, keepdims=True) + 1e-06)

        @pl.when(q == 0)
        def _():
            first_unit[...] = unit[:1]

        real = lax.broadcasted_iota(jnp.int32, (ROWS, 1), 0) + q * ROWS < length_ref[0]
        units[OWN, 0, rows] = jnp.where(real, unit, first_unit[...]).astype(BF16)
        pass_on((OWN, 0), (M1, 0), q, up)
        pass_on((OWN, 0), (P1, 0), q, down)
        pass_on((OWN, 0), (OWN, 1), q, mate)

    store = pltpu.make_async_copy(emb, embedded_out.at[0], store_sem)
    store.start()

    for k in range(SLOTS):
        for s in range(PIECES):
            if k + 1 < SLOTS:
                sent(wt.at[k, rows_of(z, s)], chain_send.at[k, s])
                if s >= PIECES // 2:
                    sent(wt.at[k, rows_of(1 - z, s)], side_send.at[k, s - PIECES // 2])
            if k == 0 or s < PIECES // 2:
                sent(wt.at[k, rows_of(z, s)], z_send.at[k, s])
        sent(part.at[k], part_send.at[k])
    sent(ctx.at[0], ctx_send)
    for k in range(len(USED)):
        sent(tokw.at[OWN, 0], tokw_send.at[k])
    for h in (0, 1):
        sent(own_piece(h)[0], first_sem.at[1, h])

    @pl.when(c == 1)
    def _():
        for h in (0, 1):
            sent(own_piece(h)[0], first_sem.at[0, h])

    def all_landed(blk, s):
        for q in range(CHUNKS):
            landed(slot(blk, s, q), unit_sem.at[blk, s, q])

    eye = lax.broadcasted_iota(jnp.int32, (SEQ, SEQ), 0) == lax.broadcasted_iota(jnp.int32, (SEQ, SEQ), 1)
    line = lax.broadcasted_iota(jnp.int32, (8, SEQ), 0)

    def two_lines(first, second):
        return jnp.where(line == 0, first, jnp.where(line == 1, second, 0.0))

    def score(sim, a, b, to_a=True):
        best_a = jnp.sum(jnp.where(eye, jnp.max(sim, axis=1, keepdims=True), 0.0), axis=0, keepdims=True)
        best_b = jnp.max(sim, axis=0, keepdims=True)
        p = jnp.sum(tokw[a[0], a[1], 0:1] * best_a, axis=1, keepdims=True)
        r = jnp.sum(tokw[b[0], b[1], 0:1] * best_b, axis=1, keepdims=True)
        lane_b = number(*b) if to_a is True else jnp.where(to_a, number(*b), -1)
        lane_a = number(*a)
        result[a[0], a[1]] = result[a[0], a[1]] + jnp.where(lane == lane_b, two_lines(p, r), 0.0)
        result[b[0], b[1]] = result[b[0], b[1]] + jnp.where(lane == lane_a, two_lines(r, p), 0.0)

    def single(blk, s, other):
        score(
            lax.dot_general(units[blk, s], units[other, 0], NT, preferred_element_type=F32), (blk, s), (other, 0)
        )

    def double(blk, s, other, keep_self=True):
        sims = lax.dot_general(
            units[blk, s], units[pl.ds(other, 2), 0].reshape(2 * SEQ, WIDTH), NT, preferred_element_type=F32
        )
        score(sims[:, :SEQ], (blk, s), (other, 0), keep_self)
        score(sims[:, SEQ:], (blk, s), (other + 1, 0))

    @pl.loop(0, 2 * CHUNKS)
    def _(t):
        @pl.when(t < CHUNKS)
        def _():
            q = t
            landed(slot(M1, 0, q), unit_sem.at[M1, 0, q])
            pass_on((M1, 0), (M2, 0), q, up)
            landed(slot(P1, 0, q), unit_sem.at[P1, 0, q])
            pass_on((P1, 0), (P2, 0), q, down)
            pass_on((P1, 0), (C1, 0), q, across)
            pass_on((M1, 0), (M1, 1), q, mate)

        @pl.when(t >= CHUNKS)
        def _():
            q = t - CHUNKS
            landed(slot(P2, 0, q), unit_sem.at[P2, 0, q])
            pass_on((P2, 0), (C2, 0), q, across)
            landed(slot(M2, 0, q), unit_sem.at[M2, 0, q])
            pass_on((M2, 0), (M2, 1), q, mate)

        @pl.when(t == 2)
        def _():
            for blk, s in USED:
                landed(tokw.at[blk, s], tokw_sem.at[blk, s])

        for when, blk, s in ((4, OWN, 1), (5, C1, 0), (6, M1, 1)):
            @pl.when(t == when)
            def _(blk=blk, s=s):
                all_landed(blk, s)

        @pl.when(t >= 3)
        def _():
            left = jnp.where(t <= 4, OWN, jnp.where(t <= 6, M1, M2))
            sample = jnp.where((t == 4) | (t == 6), 1, 0)
            double(left, sample, jnp.where(t <= 4, OWN, P1), t >= 5)

    @pl.loop(0, 3)
    def _(t):
        single(jnp.where(t < 2, OWN, P1), t % 2, C1)

    all_landed(M2, 1)
    double(M2, 1, P1)

    @pl.loop(0, 2)
    def _(t):
        @pl.when(t == 1)
        def _():
            all_landed(C2, 0)

        single(M2, jnp.where(t == 0, y // 4, 0), P2 + t)

    for k, (blk, s) in enumerate(USED):
        remote(
            result.at[blk, s], arrived.at[k], result_send.at[k], result_sem.at[k], owner(blk, s)
        ).start()
    @pl.loop(0, CHUNKS)
    def _(q):
        for m, (src, _) in enumerate(moves):
            sent(slot(*src, q), unit_send.at[m, q])

    store.wait()
    for k, (blk, s) in enumerate(USED):
        sent(result.at[blk, s], result_send.at[k])
    for k in range(len(USED)):
        landed(arrived.at[k], result_sem.at[k])
    everything = result[OWN, 0]
    for k in range(len(USED)):
        everything = everything + arrived[k]
    precision = everything[0:1]
    recall = everything[1:2]
    f_score = 2.0 * precision * recall / jnp.maximum(precision + recall, 0.25)
    others = jnp.where((lane < 32) & (lane != number(OWN, 0)), f_score, 0.0)
    utility = jnp.sum(others, axis=1, keepdims=True) / 31.0
    scores_out[...] = jnp.where(line < 2, everything, jnp.where(line == 2, f_score, utility))


def hand_out(
    embedded_ref, scores_ref, embedded_out, precision_out, recall_out, f_out, utility_out,
    emb, scores, row_p, row_r, row_f, one, load_sem, store_sem, small_sem,
):
    parts = emb.shape[0]
    rows = emb.shape[1]
    loads = [
        pltpu.make_async_copy(embedded_ref.at[0, pl.ds(k * rows, rows)], emb.at[k], load_sem.at[k])
        for k in range(parts)
    ]
    stores = [
        pltpu.make_async_copy(emb.at[k], embedded_out.at[0, pl.ds(k * rows, rows)], store_sem.at[k])
        for k in range(parts)
    ]
    load_scores = pltpu.make_async_copy(scores_ref, scores, load_sem.at[parts])
    load_scores.start()
    for load in loads:
        load.start()
    load_scores.wait()
    row_p[...] = scores[0:1, :32]
    row_r[...] = scores[1:2, :32]
    row_f[...] = scores[2:3, :32]
    one[...] = scores[3:4, :1]
    small = [
        pltpu.make_async_copy(src, dst, small_sem.at[k])
        for k, (src, dst) in enumerate(
            ((row_p, precision_out), (row_r, recall_out), (row_f, f_out), (one, utility_out))
        )
    ]
    for copy in small:
        copy.start()
    for load, store in zip(loads, stores):
        load.wait()
        store.start()
    for copy in small + stores:
        copy.wait()


def local(
    context, hidden, out_weight, out_bias, norm_gain, norm_bias, token_ids, lengths, idf_table
):
    vocab = idf_table.shape[0]
    table_rows = vocab // WIDTH * 8 + 16
    vmem = pl.BlockSpec(memory_space=pltpu.VMEM)
    hbm = pl.BlockSpec(memory_space=pl.ANY)
    dma = pltpu.SemaphoreType.DMA
    count = len(USED)
    embedded, scores = pl.pallas_call(
        kernel,
        out_shape=(
            jax.ShapeDtypeStruct((1, SEQ, WIDTH), BF16),
            jax.ShapeDtypeStruct((8, SEQ), F32),
        ),
        in_specs=[hbm] * 9,
        out_specs=(hbm, vmem),
        scratch_shapes=[
            pltpu.VMEM((2, SEQ, WIDTH), BF16),
            pltpu.VMEM((SEQ, WIDTH), BF16),
            pltpu.VMEM((SLOTS, SEQ, WIDTH), BF16),
            pltpu.VMEM((SLOTS, SEQ, SEQ), F32),
            pltpu.VMEM((SEQ, WIDTH), F32),
            pltpu.VMEM((3, 1, WIDTH), F32),
            pltpu.VMEM((1, SEQ), jnp.int32),
            pltpu.SMEM((1,), jnp.int32),
            pltpu.VMEM((vocab,), BF16),
            pltpu.VMEM((table_rows, SEQ), BF16),
            pltpu.VMEM((SEQ, WIDTH), BF16),
            pltpu.VMEM((7, 2, SEQ, WIDTH), BF16),
            pltpu.VMEM((1, WIDTH), F32),
            pltpu.VMEM((7, 2, 8, SEQ), F32),
            pltpu.VMEM((7, 2, 8, SEQ), F32),
            pltpu.VMEM((count, 8, SEQ), F32),
            dma((8,)),
            dma,
            dma((2, 2)),
            dma((SLOTS - 1, PIECES)),
            dma((SLOTS, PIECES)),
            dma((SLOTS - 1, PIECES // 2)),
            dma,
            dma((SLOTS,)),
            dma((count,)),
            dma((9, CHUNKS)),
            dma((count,)),
            dma((SLOTS, PIECES)),
            dma((SLOTS, PIECES)),
            dma,
            dma((SLOTS,)),
            dma((7, 2)),
            dma((7, 2, CHUNKS)),
            dma((count,)),
        ],
        compiler_params=pltpu.CompilerParams(
            collective_id=0, has_side_effects=True, vmem_limit_bytes=60 * 1024 * 1024
        ),
        cost_estimate=pl.CostEstimate(flops=1 << 30, bytes_accessed=1 << 20, transcendentals=0),
    )(
        context, hidden, out_weight.T, out_bias.reshape(1, WIDTH), norm_gain.reshape(1, WIDTH),
        norm_bias.reshape(1, WIDTH), token_ids, lengths, idf_table,
    )
    embedded, precision, recall, f_score, utility = pl.pallas_call(
        hand_out,
        out_shape=(
            jax.ShapeDtypeStruct((1, SEQ, WIDTH), BF16),
            jax.ShapeDtypeStruct((1, 32), F32),
            jax.ShapeDtypeStruct((1, 32), F32),
            jax.ShapeDtypeStruct((1, 32), F32),
            jax.ShapeDtypeStruct((1, 1), F32),
        ),
        in_specs=[hbm, hbm],
        out_specs=(hbm,) * 5,
        scratch_shapes=[
            pltpu.VMEM((2, SEQ // 2, WIDTH), BF16),
            pltpu.VMEM((8, SEQ), F32),
            pltpu.VMEM((1, 32), F32),
            pltpu.VMEM((1, 32), F32),
            pltpu.VMEM((1, 32), F32),
            pltpu.VMEM((1, 1), F32),
            dma((3,)),
            dma((2,)),
            dma((4,)),
        ],
        compiler_params=pltpu.CompilerParams(vmem_limit_bytes=60 * 1024 * 1024),
    )(embedded, scores)
    return embedded, precision, recall, f_score, utility.reshape(1)


def solution(mesh):
    placed = (
        P(("doc", "samp", "tok"), None, None),
        P(("doc", "samp", "tok"), None, None),
        P(None, ("samp", "tok")),
        P(),
        P(),
        P(),
        P(("doc", "samp", "tok"), None),
        P(("doc", "samp", "tok")),
        P(),
    )
    return jax.shard_map(
        local,
        mesh=mesh,
        in_specs=placed,
        out_specs=(
            P(("doc", "samp", "tok"), None, None),
            P(("doc", "samp", "tok"), None),
            P(("doc", "samp", "tok"), None),
            P(("doc", "samp", "tok"), None),
            P(("doc", "samp", "tok")),
        ),
        check_vma=False,
    )
```

```python
import jax
import jax.numpy as jnp
from jax import lax
from jax.experimental import pallas as pl
from jax.experimental.pallas import tpu as pltpu
from jax.sharding import PartitionSpec as P

MESH = pl.DeviceIdType.MESH
F32 = jnp.float32
BF16 = jnp.bfloat16

SEQ = 128
WIDTH = 1024
RING = 8
SLICE = 32
SLOTS = 4
PIECE = 16
PIECES = 2 * SLICE // PIECE
CHUNKS = 4
ROWS = SEQ // CHUNKS
NT = (((1,), (1,)), ((), ()))

OWN, M1, M2, P1, C1, P2, C2 = range(7)
PLACES = {OWN: (0, 0), M1: (-1, 0), M2: (-2, 0), P1: (1, 0), C1: (1, 1), P2: (2, 0), C2: (2, 1)}
USED = [(OWN, 1), (M1, 0), (M1, 1), (M2, 0), (M2, 1), (P1, 0), (C1, 0), (P2, 0), (C2, 0)]


def kernel(
    context_hbm, hidden_hbm, weight_hbm, bias_hbm, gain_hbm, shift_hbm, ids_hbm, length_hbm, table_hbm,
    embedded_out, scores_out,
    ctx, hid, wt, part, mixed, params, ids_ref, length_ref, flat, table, emb, units, first_unit, tokw, result, arrived,
    load_sem, store_sem, first_sem, chain_send, z_send, side_send, ctx_send, part_send, tokw_send, unit_send, result_send,
    slice_sem, z_sem, ctx_sem, part_sem, tokw_sem, unit_sem, result_sem,
):
    doc = lax.axis_index("doc")
    y = lax.axis_index("samp")
    tok = lax.axis_index("tok")
    z, c = tok // 2, tok % 2

    def device(dy, flip_z, flip_c):
        yy = (y + dy + RING) % RING
        zz = 1 - z if flip_z else z
        return (doc, yy, zz * 2 + (c + flip_c) % 2)

    def holder(blk, s):
        dy, flip_z = PLACES[blk]
        return device(-dy, flip_z, s + (1 - z if flip_z else 0))

    def owner(blk, s):
        dy, flip_z = PLACES[blk]
        return device(dy, flip_z, s + (z if flip_z else 0))

    def number(blk, s):
        dy = jnp.where(blk <= M2, -blk, (blk - 1) // 2)
        flip = jnp.where((blk == C1) | (blk == C2), 1, 0)
        return (y + dy + RING) % RING * 4 + (z + flip) % 2 * 2 + (c + s + flip * z) % 2

    up, down, inner, mate = device(1, 0, 0), device(-1, 0, 0), device(0, 1, 0), device(0, 0, 1)
    ahead = device(1 - 2 * c, 0, 0)
    across = device(0, 1, 1 - z)

    def rows_of(zz, piece):
        return pl.ds(pl.multiple_of(zz * 2 * SLICE + piece * PIECE, PIECE), PIECE)

    partners = [inner, device(0, 1, 1), mate]
    partners += [device(dy, 0, fc) for dy in (1, -1, 2, -2) for fc in (0, 1)]
    partners += [device(dy, 1, z) for dy in (1, 2)]
    partners += [device(dy, 1, 1 - z) for dy in (-1, -2)]
    barrier = pltpu.get_barrier_semaphore()
    for partner in partners:
        pl.semaphore_signal(barrier, inc=1, device_id=partner, device_id_type=MESH)

    def own_piece(h):
        return weight_hbm.at[pl.ds(h * PIECE, PIECE)], wt.at[0, rows_of(z, c * 2 + h)]

    @pl.when(c == 0)
    def _():
        for h in (0, 1):
            pltpu.make_async_copy(*own_piece(h), slice_sem.at[0, h]).start()

    loads = [
        pltpu.make_async_copy(context_hbm.at[0], ctx.at[0], load_sem.at[0]),
        pltpu.make_async_copy(table_hbm, flat, load_sem.at[1]),
        pltpu.make_async_copy(ids_hbm, ids_ref, load_sem.at[2]),
        pltpu.make_async_copy(length_hbm, length_ref, load_sem.at[3]),
        pltpu.make_async_copy(hidden_hbm.at[0], hid, load_sem.at[4]),
        pltpu.make_async_copy(bias_hbm, params.at[0], load_sem.at[5]),
        pltpu.make_async_copy(gain_hbm, params.at[1], load_sem.at[6]),
        pltpu.make_async_copy(shift_hbm, params.at[2], load_sem.at[7]),
    ]
    for load in loads:
        load.start()

    def remote(src, dst, send_sem, recv_sem, target):
        return pltpu.make_async_remote_copy(
            src_ref=src, dst_ref=dst, send_sem=send_sem, recv_sem=recv_sem,
            device_id=target, device_id_type=MESH,
        )

    def landed(dst, recv_sem):
        remote(dst, dst, ctx_send, recv_sem, mate).wait_recv()

    def sent(src, send_sem):
        remote(src, src, send_sem, ctx_sem, mate).wait_send()

    result[...] = jnp.zeros_like(result)
    pl.semaphore_wait(barrier, len(partners))

    below = (doc, (y + RING - 1) % RING, z * 2 + 1)

    for h in (0, 1):
        @pl.when(c == 0)
        def _(h=h):
            remote(*own_piece(h), first_sem.at[1, h], slice_sem.at[0, h], below).start()

        @pl.when(c == 1)
        def _(h=h):
            remote(*own_piece(h), first_sem.at[1, h], slice_sem.at[0, 2 + h], below).start()
            remote(*own_piece(h), first_sem.at[0, h], slice_sem.at[0, 2 + h], mate).start()

    loads[0].wait()
    remote(ctx.at[0], ctx.at[1], ctx_send, ctx_sem, mate).start()

    def columns_at(k, core):
        yy = (y + RING + jnp.where(core == 0, -k, k + 1)) % RING
        return pl.ds(pl.multiple_of(yy * SEQ, SEQ), SEQ)

    lane = lax.broadcasted_iota(jnp.int32, (1, SEQ), 1)

    def token_weights():
        for load in loads[1:4]:
            load.wait()
        vocab = flat.shape[0]
        full = vocab // WIDTH
        table[pl.ds(full * 8, 16)] = jnp.zeros((16, SEQ), BF16)

        @pl.loop(0, full)
        def _(k):
            table[pl.ds(pl.multiple_of(k * 8, 8), 8)] = flat[
                pl.ds(pl.multiple_of(k * WIDTH, WIDTH), WIDTH)
            ].reshape(8, SEQ)

        for k in range(full * 8, -(-vocab // SEQ)):
            count = min(SEQ, vocab - k * SEQ)
            table[k:k + 1, :count] = flat[pl.ds(k * SEQ, count)].reshape(1, count)
        ids = ids_ref[...]
        chosen = lax.broadcasted_iota(jnp.int32, (SEQ, SEQ), 0) == (ids & (SEQ - 1))
        columns = jnp.dot(
            table[...], jnp.where(chosen, 1.0, 0.0).astype(BF16), preferred_element_type=F32
        )
        row_hit = lax.broadcasted_iota(jnp.int32, columns.shape, 0) == (ids >> 7)
        found = jnp.sum(jnp.where(row_hit, columns, 0.0), axis=0, keepdims=True)
        own = jnp.where(lane < length_ref[0], found, 0.0)
        own = own / jnp.sum(own, axis=1, keepdims=True)
        tokw[OWN, 0] = jnp.broadcast_to(own, (8, SEQ))

    def send_token_weights():
        for k, (blk, s) in enumerate(USED):
            remote(
                tokw.at[OWN, 0], tokw.at[blk, s], tokw_send.at[k], tokw_sem.at[blk, s], holder(blk, s)
            ).start()

    @pl.loop(0, SLOTS + 1)
    def _(k):
        @pl.when(k < SLOTS)
        def _():
            for s in range(PIECES):
                rows = rows_of(z, s)
                landed(wt.at[k, rows], slice_sem.at[k, s])

                @pl.when(k + 1 < SLOTS)
                def _(rows=rows, s=s):
                    remote(
                        wt.at[k, rows], wt.at[k + 1, rows], chain_send.at[k, s], slice_sem.at[k + 1, s], ahead
                    ).start()

                @pl.when((k == 0) | (s < PIECES // 2))
                def _(rows=rows, s=s):
                    remote(wt.at[k, rows], wt.at[k, rows], z_send.at[k, s], z_sem.at[k, s], inner).start()

        @pl.when(k >= 1)
        def _():
            for s in range(PIECES // 2, PIECES):
                rows = rows_of(1 - z, s)
                landed(wt.at[k - 1, rows], z_sem.at[k - 1, s])

                @pl.when(k < SLOTS)
                def _(rows=rows, s=s):
                    remote(
                        wt.at[k - 1, rows], wt.at[k, rows], side_send.at[k - 1, s - PIECES // 2], z_sem.at[k, s], ahead
                    ).start()

        @pl.when(k == 3)
        def _():
            landed(ctx.at[1], ctx_sem)

        @pl.when(k >= 3)
        def _():
            first = (k - 3) * 2
            for n in (0, 1):
                for s in range(PIECES // 2):
                    landed(wt.at[first + n, rows_of(1 - z, s)], z_sem.at[first + n, s])
            both = lax.dot_general(
                ctx[...].reshape(2 * SEQ, WIDTH), wt[pl.ds(first, 2)].reshape(2 * SEQ, WIDTH), NT,
                preferred_element_type=F32,
            )
            for n in (0, 1):
                at = columns_at(first + n, c)
                side = slice(n * SEQ, (n + 1) * SEQ)
                part[first + n] = both[SEQ:, side]
                remote(
                    part.at[first + n], mixed.at[:, at], part_send.at[first + n], part_sem.at[first + n], mate
                ).start()
                mixed[:, at] = both[:SEQ, side]

        @pl.when(k == 0)
        def _():
            token_weights()

        @pl.when(k == 1)
        def _():
            send_token_weights()

    for load in loads[4:]:
        load.wait()
    for k in range(SLOTS):
        landed(mixed.at[:, columns_at(k, 1 - c)], part_sem.at[k])

    def slot(blk, s, q):
        return units.at[blk, s, pl.ds(pl.multiple_of(q * ROWS, ROWS), ROWS)]

    moves = []

    def pass_on(src, dst, q, target):
        if (src, dst) not in moves:
            moves.append((src, dst))
        remote(
            slot(*src, q), slot(*dst, q), unit_send.at[moves.index((src, dst)), q],
            unit_sem.at[dst[0], dst[1], q], target,
        ).start()

    @pl.loop(0, CHUNKS)
    def _(q):
        rows = pl.ds(pl.multiple_of(q * ROWS, ROWS), ROWS)
        x = hid[rows, :].astype(F32) + mixed[rows, :] + params[0]
        centre = x - jnp.mean(x, axis=-1, keepdims=True)
        spread = jnp.mean(centre * centre, axis=-1, keepdims=True)
        embedded = (centre * lax.rsqrt(spread + 1e-07) * params[1] + params[2]).astype(BF16)
        emb[rows, :] = embedded
        values = embedded.astype(F32)
        unit = values * lax.rsqrt(jnp.sum(values * values, axis=-1, keepdims=True) + 1e-06)

        @pl.when(q == 0)
        def _():
            first_unit[...] = unit[:1]

        real = lax.broadcasted_iota(jnp.int32, (ROWS, 1), 0) + q * ROWS < length_ref[0]
        units[OWN, 0, rows] = jnp.where(real, unit, first_unit[...]).astype(BF16)
        pass_on((OWN, 0), (M1, 0), q, up)
        pass_on((OWN, 0), (P1, 0), q, down)
        pass_on((OWN, 0), (OWN, 1), q, mate)

    store = pltpu.make_async_copy(emb, embedded_out.at[0], store_sem)
    store.start()

    for k in range(SLOTS):
        for s in range(PIECES):
            if k + 1 < SLOTS:
                sent(wt.at[k, rows_of(z, s)], chain_send.at[k, s])
                if s >= PIECES // 2:
                    sent(wt.at[k, rows_of(1 - z, s)], side_send.at[k, s - PIECES // 2])
            if k == 0 or s < PIECES // 2:
                sent(wt.at[k, rows_of(z, s)], z_send.at[k, s])
        sent(part.at[k], part_send.at[k])
    sent(ctx.at[0], ctx_send)
    for k, (blk, s) in enumerate(USED):
        sent(tokw.at[OWN, 0], tokw_send.at[k])
        landed(tokw.at[blk, s], tokw_sem.at[blk, s])
    for h in (0, 1):
        sent(own_piece(h)[0], first_sem.at[1, h])

    @pl.when(c == 1)
    def _():
        for h in (0, 1):
            sent(own_piece(h)[0], first_sem.at[0, h])

    def all_landed(blk, s):
        for q in range(CHUNKS):
            landed(slot(blk, s, q), unit_sem.at[blk, s, q])

    eye = lax.broadcasted_iota(jnp.int32, (SEQ, SEQ), 0) == lax.broadcasted_iota(jnp.int32, (SEQ, SEQ), 1)
    line = lax.broadcasted_iota(jnp.int32, (8, SEQ), 0)

    def two_lines(first, second):
        return jnp.where(line == 0, first, jnp.where(line == 1, second, 0.0))

    def score(sim, a, b, to_a=True):
        best_a = jnp.sum(jnp.where(eye, jnp.max(sim, axis=1, keepdims=True), 0.0), axis=0, keepdims=True)
        best_b = jnp.max(sim, axis=0, keepdims=True)
        p = jnp.sum(tokw[a[0], a[1], 0:1] * best_a, axis=1, keepdims=True)
        r = jnp.sum(tokw[b[0], b[1], 0:1] * best_b, axis=1, keepdims=True)
        lane_b = number(*b) if to_a is True else jnp.where(to_a, number(*b), -1)
        lane_a = number(*a)
        result[a[0], a[1]] = result[a[0], a[1]] + jnp.where(lane == lane_b, two_lines(p, r), 0.0)
        result[b[0], b[1]] = result[b[0], b[1]] + jnp.where(lane == lane_a, two_lines(r, p), 0.0)

    def single(blk, s, other):
        score(
            lax.dot_general(units[blk, s], units[other, 0], NT, preferred_element_type=F32), (blk, s), (other, 0)
        )

    def double(blk, s, other, keep_self=True):
        sims = lax.dot_general(
            units[blk, s], units[pl.ds(other, 2), 0].reshape(2 * SEQ, WIDTH), NT, preferred_element_type=F32
        )
        score(sims[:, :SEQ], (blk, s), (other, 0), keep_self)
        score(sims[:, SEQ:], (blk, s), (other + 1, 0))

    @pl.loop(0, 2 * CHUNKS)
    def _(t):
        @pl.when(t < CHUNKS)
        def _():
            q = t
            landed(slot(M1, 0, q), unit_sem.at[M1, 0, q])
            pass_on((M1, 0), (M2, 0), q, up)
            landed(slot(P1, 0, q), unit_sem.at[P1, 0, q])
            pass_on((P1, 0), (P2, 0), q, down)
            pass_on((P1, 0), (C1, 0), q, across)
            pass_on((M1, 0), (M1, 1), q, mate)

        @pl.when(t >= CHUNKS)
        def _():
            q = t - CHUNKS
            landed(slot(P2, 0, q), unit_sem.at[P2, 0, q])
            pass_on((P2, 0), (C2, 0), q, across)
            landed(slot(M2, 0, q), unit_sem.at[M2, 0, q])
            pass_on((M2, 0), (M2, 1), q, mate)

        for when, blk, s in ((4, OWN, 1), (5, C1, 0), (6, M1, 1)):
            @pl.when(t == when)
            def _(blk=blk, s=s):
                all_landed(blk, s)

        @pl.when(t >= 3)
        def _():
            left = jnp.where(t <= 4, OWN, jnp.where(t <= 6, M1, M2))
            sample = jnp.where((t == 4) | (t == 6), 1, 0)
            double(left, sample, jnp.where(t <= 4, OWN, P1), t >= 5)

    @pl.loop(0, 3)
    def _(t):
        single(jnp.where(t < 2, OWN, P1), t % 2, C1)

    all_landed(M2, 1)
    double(M2, 1, P1)

    @pl.loop(0, 2)
    def _(t):
        @pl.when(t == 1)
        def _():
            all_landed(C2, 0)

        single(M2, jnp.where(t == 0, y // 4, 0), P2 + t)

    for k, (blk, s) in enumerate(USED):
        remote(
            result.at[blk, s], arrived.at[k], result_send.at[k], result_sem.at[k], owner(blk, s)
        ).start()
    @pl.loop(0, CHUNKS)
    def _(q):
        for m, (src, _) in enumerate(moves):
            sent(slot(*src, q), unit_send.at[m, q])

    store.wait()
    for k, (blk, s) in enumerate(USED):
        sent(result.at[blk, s], result_send.at[k])
    for k in range(len(USED)):
        landed(arrived.at[k], result_sem.at[k])
    everything = result[OWN, 0]
    for k in range(len(USED)):
        everything = everything + arrived[k]
    precision = everything[0:1]
    recall = everything[1:2]
    f_score = 2.0 * precision * recall / jnp.maximum(precision + recall, 0.25)
    others = jnp.where((lane < 32) & (lane != number(OWN, 0)), f_score, 0.0)
    utility = jnp.sum(others, axis=1, keepdims=True) / 31.0
    scores_out[...] = jnp.where(line < 2, everything, jnp.where(line == 2, f_score, utility))


def hand_out(
    embedded_ref, scores_ref, embedded_out, precision_out, recall_out, f_out, utility_out,
    emb, scores, row_p, row_r, row_f, one, load_sem, store_sem, small_sem,
):
    parts = emb.shape[0]
    rows = emb.shape[1]
    loads = [
        pltpu.make_async_copy(embedded_ref.at[0, pl.ds(k * rows, rows)], emb.at[k], load_sem.at[k])
        for k in range(parts)
    ]
    stores = [
        pltpu.make_async_copy(emb.at[k], embedded_out.at[0, pl.ds(k * rows, rows)], store_sem.at[k])
        for k in range(parts)
    ]
    load_scores = pltpu.make_async_copy(scores_ref, scores, load_sem.at[parts])
    load_scores.start()
    for load in loads:
        load.start()
    load_scores.wait()
    row_p[...] = scores[0:1, :32]
    row_r[...] = scores[1:2, :32]
    row_f[...] = scores[2:3, :32]
    one[...] = scores[3:4, :1]
    small = [
        pltpu.make_async_copy(src, dst, small_sem.at[k])
        for k, (src, dst) in enumerate(
            ((row_p, precision_out), (row_r, recall_out), (row_f, f_out), (one, utility_out))
        )
    ]
    for copy in small:
        copy.start()
    for load, store in zip(loads, stores):
        load.wait()
        store.start()
    for copy in small + stores:
        copy.wait()


def local(
    context, hidden, out_weight, out_bias, norm_gain, norm_bias, token_ids, lengths, idf_table
):
    vocab = idf_table.shape[0]
    table_rows = vocab // WIDTH * 8 + 16
    vmem = pl.BlockSpec(memory_space=pltpu.VMEM)
    hbm = pl.BlockSpec(memory_space=pl.ANY)
    dma = pltpu.SemaphoreType.DMA
    count = len(USED)
    embedded, scores = pl.pallas_call(
        kernel,
        out_shape=(
            jax.ShapeDtypeStruct((1, SEQ, WIDTH), BF16),
            jax.ShapeDtypeStruct((8, SEQ), F32),
        ),
        in_specs=[hbm] * 9,
        out_specs=(hbm, vmem),
        scratch_shapes=[
            pltpu.VMEM((2, SEQ, WIDTH), BF16),
            pltpu.VMEM((SEQ, WIDTH), BF16),
            pltpu.VMEM((SLOTS, SEQ, WIDTH), BF16),
            pltpu.VMEM((SLOTS, SEQ, SEQ), F32),
            pltpu.VMEM((SEQ, WIDTH), F32),
            pltpu.VMEM((3, 1, WIDTH), F32),
            pltpu.VMEM((1, SEQ), jnp.int32),
            pltpu.SMEM((1,), jnp.int32),
            pltpu.VMEM((vocab,), BF16),
            pltpu.VMEM((table_rows, SEQ), BF16),
            pltpu.VMEM((SEQ, WIDTH), BF16),
            pltpu.VMEM((7, 2, SEQ, WIDTH), BF16),
            pltpu.VMEM((1, WIDTH), F32),
            pltpu.VMEM((7, 2, 8, SEQ), F32),
            pltpu.VMEM((7, 2, 8, SEQ), F32),
            pltpu.VMEM((count, 8, SEQ), F32),
            dma((8,)),
            dma,
            dma((2, 2)),
            dma((SLOTS - 1, PIECES)),
            dma((SLOTS, PIECES)),
            dma((SLOTS - 1, PIECES // 2)),
            dma,
            dma((SLOTS,)),
            dma((count,)),
            dma((9, CHUNKS)),
            dma((count,)),
            dma((SLOTS, PIECES)),
            dma((SLOTS, PIECES)),
            dma,
            dma((SLOTS,)),
            dma((7, 2)),
            dma((7, 2, CHUNKS)),
            dma((count,)),
        ],
        compiler_params=pltpu.CompilerParams(
            collective_id=0, has_side_effects=True, vmem_limit_bytes=60 * 1024 * 1024
        ),
        cost_estimate=pl.CostEstimate(flops=1 << 30, bytes_accessed=1 << 20, transcendentals=0),
    )(
        context, hidden, out_weight.T, out_bias.reshape(1, WIDTH), norm_gain.reshape(1, WIDTH),
        norm_bias.reshape(1, WIDTH), token_ids, lengths, idf_table,
    )
    embedded, precision, recall, f_score, utility = pl.pallas_call(
        hand_out,
        out_shape=(
            jax.ShapeDtypeStruct((1, SEQ, WIDTH), BF16),
            jax.ShapeDtypeStruct((1, 32), F32),
            jax.ShapeDtypeStruct((1, 32), F32),
            jax.ShapeDtypeStruct((1, 32), F32),
            jax.ShapeDtypeStruct((1, 1), F32),
        ),
        in_specs=[hbm, hbm],
        out_specs=(hbm,) * 5,
        scratch_shapes=[
            pltpu.VMEM((2, SEQ // 2, WIDTH), BF16),
            pltpu.VMEM((8, SEQ), F32),
            pltpu.VMEM((1, 32), F32),
            pltpu.VMEM((1, 32), F32),
            pltpu.VMEM((1, 32), F32),
            pltpu.VMEM((1, 1), F32),
            dma((3,)),
            dma((2,)),
            dma((4,)),
        ],
        compiler_params=pltpu.CompilerParams(vmem_limit_bytes=60 * 1024 * 1024),
    )(embedded, scores)
    return embedded, precision, recall, f_score, utility.reshape(1)


def solution(mesh):
    placed = (
        P(("doc", "samp", "tok"), None, None),
        P(("doc", "samp", "tok"), None, None),
        P(None, ("samp", "tok")),
        P(),
        P(),
        P(),
        P(("doc", "samp", "tok"), None),
        P(("doc", "samp", "tok")),
        P(),
    )
    return jax.shard_map(
        local,
        mesh=mesh,
        in_specs=placed,
        out_specs=(
            P(("doc", "samp", "tok"), None, None),
            P(("doc", "samp", "tok"), None),
            P(("doc", "samp", "tok"), None),
            P(("doc", "samp", "tok"), None),
            P(("doc", "samp", "tok")),
        ),
        check_vma=False,
    )
```

```python
import jax
import jax.numpy as jnp
from jax import lax
from jax.experimental import pallas as pl
from jax.experimental.pallas import tpu as pltpu
from jax.sharding import PartitionSpec as P

MESH = pl.DeviceIdType.MESH
F32 = jnp.float32
BF16 = jnp.bfloat16

SEQ = 128
WIDTH = 1024
RING = 8
SLICE = 32
SLOTS = 4
PIECE = 16
PIECES = 2 * SLICE // PIECE
CHUNKS = 4
ROWS = SEQ // CHUNKS
NT = (((1,), (1,)), ((), ()))

OWN, M1, M2, P1, C1, P2, C2 = range(7)
PLACES = {OWN: (0, 0), M1: (-1, 0), M2: (-2, 0), P1: (1, 0), C1: (1, 1), P2: (2, 0), C2: (2, 1)}
USED = [(OWN, 1), (M1, 0), (M1, 1), (M2, 0), (M2, 1), (P1, 0), (C1, 0), (P2, 0), (C2, 0)]


def kernel(
    context_hbm, hidden_hbm, weight_hbm, bias_hbm, gain_hbm, shift_hbm, ids_hbm, length_hbm, table_hbm,
    embedded_out, scores_out,
    ctx, hid, wt, part, mixed, params, ids_ref, length_ref, flat, table, emb, units, first_unit, tokw, result, arrived,
    load_sem, store_sem, first_sem, chain_send, z_send, side_send, ctx_send, part_send, tokw_send, unit_send, result_send,
    slice_sem, z_sem, ctx_sem, part_sem, tokw_sem, unit_sem, result_sem,
):
    doc = lax.axis_index("doc")
    y = lax.axis_index("samp")
    tok = lax.axis_index("tok")
    z, c = tok // 2, tok % 2

    def device(dy, flip_z, flip_c):
        yy = (y + dy + RING) % RING
        zz = 1 - z if flip_z else z
        return (doc, yy, zz * 2 + (c + flip_c) % 2)

    def holder(blk, s):
        dy, flip_z = PLACES[blk]
        return device(-dy, flip_z, s + (1 - z if flip_z else 0))

    def owner(blk, s):
        dy, flip_z = PLACES[blk]
        return device(dy, flip_z, s + (z if flip_z else 0))

    def number(blk, s):
        dy = jnp.where(blk <= M2, -blk, (blk - 1) // 2)
        flip = jnp.where((blk == C1) | (blk == C2), 1, 0)
        return (y + dy + RING) % RING * 4 + (z + flip) % 2 * 2 + (c + s + flip * z) % 2

    up, down, inner, mate = device(1, 0, 0), device(-1, 0, 0), device(0, 1, 0), device(0, 0, 1)
    ahead = device(1 - 2 * c, 0, 0)
    across = device(0, 1, 1 - z)

    def rows_of(zz, piece):
        return pl.ds(pl.multiple_of(zz * 2 * SLICE + piece * PIECE, PIECE), PIECE)

    def own_piece(h):
        return weight_hbm.at[pl.ds(h * PIECE, PIECE)], wt.at[0, rows_of(z, c * 2 + h)]

    @pl.when(c == 0)
    def _():
        for h in (0, 1):
            pltpu.make_async_copy(*own_piece(h), slice_sem.at[0, h]).start()

    loads = [
        pltpu.make_async_copy(context_hbm.at[0], ctx.at[0], load_sem.at[0]),
        pltpu.make_async_copy(table_hbm, flat, load_sem.at[1]),
        pltpu.make_async_copy(ids_hbm, ids_ref, load_sem.at[2]),
        pltpu.make_async_copy(length_hbm, length_ref, load_sem.at[3]),
        pltpu.make_async_copy(hidden_hbm.at[0], hid, load_sem.at[4]),
        pltpu.make_async_copy(bias_hbm, params.at[0], load_sem.at[5]),
        pltpu.make_async_copy(gain_hbm, params.at[1], load_sem.at[6]),
        pltpu.make_async_copy(shift_hbm, params.at[2], load_sem.at[7]),
    ]
    for load in loads:
        load.start()

    partners = [inner, device(0, 1, 1), mate]
    partners += [device(dy, 0, fc) for dy in (1, -1, 2, -2) for fc in (0, 1)]
    partners += [device(dy, 1, z) for dy in (1, 2)]
    partners += [device(dy, 1, 1 - z) for dy in (-1, -2)]
    barrier = pltpu.get_barrier_semaphore()
    for partner in partners:
        pl.semaphore_signal(barrier, inc=1, device_id=partner, device_id_type=MESH)

    def remote(src, dst, send_sem, recv_sem, target):
        return pltpu.make_async_remote_copy(
            src_ref=src, dst_ref=dst, send_sem=send_sem, recv_sem=recv_sem,
            device_id=target, device_id_type=MESH,
        )

    def landed(dst, recv_sem):
        remote(dst, dst, ctx_send, recv_sem, mate).wait_recv()

    def sent(src, send_sem):
        remote(src, src, send_sem, ctx_sem, mate).wait_send()

    result[...] = jnp.zeros_like(result)
    pl.semaphore_wait(barrier, len(partners))

    below = (doc, (y + RING - 1) % RING, z * 2 + 1)

    for h in (0, 1):
        @pl.when(c == 0)
        def _(h=h):
            remote(*own_piece(h), first_sem.at[1, h], slice_sem.at[0, h], below).start()

        @pl.when(c == 1)
        def _(h=h):
            remote(*own_piece(h), first_sem.at[1, h], slice_sem.at[0, 2 + h], below).start()
            remote(*own_piece(h), first_sem.at[0, h], slice_sem.at[0, 2 + h], mate).start()

    loads[0].wait()
    remote(ctx.at[0], ctx.at[1], ctx_send, ctx_sem, mate).start()

    def columns_at(k, core):
        yy = (y + RING + jnp.where(core == 0, -k, k + 1)) % RING
        return pl.ds(pl.multiple_of(yy * SEQ, SEQ), SEQ)

    lane = lax.broadcasted_iota(jnp.int32, (1, SEQ), 1)

    def token_weights():
        for load in loads[1:4]:
            load.wait()
        vocab = flat.shape[0]
        full = vocab // WIDTH
        table[pl.ds(full * 8, 16)] = jnp.zeros((16, SEQ), BF16)

        @pl.loop(0, full)
        def _(k):
            table[pl.ds(pl.multiple_of(k * 8, 8), 8)] = flat[
                pl.ds(pl.multiple_of(k * WIDTH, WIDTH), WIDTH)
            ].reshape(8, SEQ)

        for k in range(full * 8, -(-vocab // SEQ)):
            count = min(SEQ, vocab - k * SEQ)
            table[k:k + 1, :count] = flat[pl.ds(k * SEQ, count)].reshape(1, count)
        ids = ids_ref[...]
        chosen = lax.broadcasted_iota(jnp.int32, (SEQ, SEQ), 0) == (ids & (SEQ - 1))
        columns = jnp.dot(
            table[...], jnp.where(chosen, 1.0, 0.0).astype(BF16), preferred_element_type=F32
        )
        row_hit = lax.broadcasted_iota(jnp.int32, columns.shape, 0) == (ids >> 7)
        found = jnp.sum(jnp.where(row_hit, columns, 0.0), axis=0, keepdims=True)
        own = jnp.where(lane < length_ref[0], found, 0.0)
        own = own / jnp.sum(own, axis=1, keepdims=True)
        tokw[OWN, 0] = jnp.broadcast_to(own, (8, SEQ))
        for k, (blk, s) in enumerate(USED):
            remote(
                tokw.at[OWN, 0], tokw.at[blk, s], tokw_send.at[k], tokw_sem.at[blk, s], holder(blk, s)
            ).start()

    @pl.loop(0, SLOTS + 1)
    def _(k):
        @pl.when(k < SLOTS)
        def _():
            for s in range(PIECES):
                rows = rows_of(z, s)
                landed(wt.at[k, rows], slice_sem.at[k, s])

                @pl.when(k + 1 < SLOTS)
                def _(rows=rows, s=s):
                    remote(
                        wt.at[k, rows], wt.at[k + 1, rows], chain_send.at[k, s], slice_sem.at[k + 1, s], ahead
                    ).start()

                @pl.when((k == 0) | (s < PIECES // 2))
                def _(rows=rows, s=s):
                    remote(wt.at[k, rows], wt.at[k, rows], z_send.at[k, s], z_sem.at[k, s], inner).start()

        @pl.when(k >= 1)
        def _():
            for s in range(PIECES // 2, PIECES):
                rows = rows_of(1 - z, s)
                landed(wt.at[k - 1, rows], z_sem.at[k - 1, s])

                @pl.when(k < SLOTS)
                def _(rows=rows, s=s):
                    remote(
                        wt.at[k - 1, rows], wt.at[k, rows], side_send.at[k - 1, s - PIECES // 2], z_sem.at[k, s], ahead
                    ).start()

        @pl.when(k == 3)
        def _():
            landed(ctx.at[1], ctx_sem)

        @pl.when(k >= 3)
        def _():
            first = (k - 3) * 2
            for n in (0, 1):
                for s in range(PIECES // 2):
                    landed(wt.at[first + n, rows_of(1 - z, s)], z_sem.at[first + n, s])
            columns = wt[pl.ds(first, 2)].reshape(2 * SEQ, WIDTH)
            theirs = lax.dot_general(ctx[1], columns, NT, preferred_element_type=F32)
            for n in (0, 1):
                part[first + n] = theirs[:, n * SEQ:(n + 1) * SEQ]
                remote(
                    part.at[first + n], mixed.at[:, columns_at(first + n, c)], part_send.at[first + n],
                    part_sem.at[first + n], mate,
                ).start()
            mine = lax.dot_general(ctx[0], columns, NT, preferred_element_type=F32)
            for n in (0, 1):
                mixed[:, columns_at(first + n, c)] = mine[:, n * SEQ:(n + 1) * SEQ]

        @pl.when(k == 3)
        def _():
            token_weights()

    for load in loads[4:]:
        load.wait()
    for k in range(SLOTS):
        landed(mixed.at[:, columns_at(k, 1 - c)], part_sem.at[k])

    def slot(blk, s, q):
        return units.at[blk, s, pl.ds(pl.multiple_of(q * ROWS, ROWS), ROWS)]

    moves = []

    def pass_on(src, dst, q, target):
        if (src, dst) not in moves:
            moves.append((src, dst))
        remote(
            slot(*src, q), slot(*dst, q), unit_send.at[moves.index((src, dst)), q],
            unit_sem.at[dst[0], dst[1], q], target,
        ).start()

    @pl.loop(0, CHUNKS)
    def _(q):
        rows = pl.ds(pl.multiple_of(q * ROWS, ROWS), ROWS)
        x = hid[rows, :].astype(F32) + mixed[rows, :] + params[0]
        centre = x - jnp.mean(x, axis=-1, keepdims=True)
        spread = jnp.mean(centre * centre, axis=-1, keepdims=True)
        embedded = (centre * lax.rsqrt(spread + 1e-07) * params[1] + params[2]).astype(BF16)
        emb[rows, :] = embedded
        values = embedded.astype(F32)
        unit = values * lax.rsqrt(jnp.sum(values * values, axis=-1, keepdims=True) + 1e-06)

        @pl.when(q == 0)
        def _():
            first_unit[...] = unit[:1]

        real = lax.broadcasted_iota(jnp.int32, (ROWS, 1), 0) + q * ROWS < length_ref[0]
        units[OWN, 0, rows] = jnp.where(real, unit, first_unit[...]).astype(BF16)
        pass_on((OWN, 0), (M1, 0), q, up)
        pass_on((OWN, 0), (P1, 0), q, down)
        pass_on((OWN, 0), (OWN, 1), q, mate)

    store = pltpu.make_async_copy(emb, embedded_out.at[0], store_sem)
    store.start()

    for k in range(SLOTS):
        for s in range(PIECES):
            if k + 1 < SLOTS:
                sent(wt.at[k, rows_of(z, s)], chain_send.at[k, s])
                if s >= PIECES // 2:
                    sent(wt.at[k, rows_of(1 - z, s)], side_send.at[k, s - PIECES // 2])
            if k == 0 or s < PIECES // 2:
                sent(wt.at[k, rows_of(z, s)], z_send.at[k, s])
        sent(part.at[k], part_send.at[k])
    sent(ctx.at[0], ctx_send)
    for k in range(len(USED)):
        sent(tokw.at[OWN, 0], tokw_send.at[k])
    for h in (0, 1):
        sent(own_piece(h)[0], first_sem.at[1, h])

    @pl.when(c == 1)
    def _():
        for h in (0, 1):
            sent(own_piece(h)[0], first_sem.at[0, h])

    def all_landed(blk, s):
        for q in range(CHUNKS):
            landed(slot(blk, s, q), unit_sem.at[blk, s, q])

    eye = lax.broadcasted_iota(jnp.int32, (SEQ, SEQ), 0) == lax.broadcasted_iota(jnp.int32, (SEQ, SEQ), 1)
    line = lax.broadcasted_iota(jnp.int32, (8, SEQ), 0)

    def two_lines(first, second):
        return jnp.where(line == 0, first, jnp.where(line == 1, second, 0.0))

    def score(sim, a, b, to_a=True):
        best_a = jnp.sum(jnp.where(eye, jnp.max(sim, axis=1, keepdims=True), 0.0), axis=0, keepdims=True)
        best_b = jnp.max(sim, axis=0, keepdims=True)
        p = jnp.sum(tokw[a[0], a[1], 0:1] * best_a, axis=1, keepdims=True)
        r = jnp.sum(tokw[b[0], b[1], 0:1] * best_b, axis=1, keepdims=True)
        lane_b = number(*b) if to_a is True else jnp.where(to_a, number(*b), -1)
        lane_a = number(*a)
        result[a[0], a[1]] = result[a[0], a[1]] + jnp.where(lane == lane_b, two_lines(p, r), 0.0)
        result[b[0], b[1]] = result[b[0], b[1]] + jnp.where(lane == lane_a, two_lines(r, p), 0.0)

    def single(blk, s, other):
        score(
            lax.dot_general(units[blk, s], units[other, 0], NT, preferred_element_type=F32), (blk, s), (other, 0)
        )

    def double(blk, s, other, keep_self=True):
        sims = lax.dot_general(
            units[blk, s], units[pl.ds(other, 2), 0].reshape(2 * SEQ, WIDTH), NT, preferred_element_type=F32
        )
        score(sims[:, :SEQ], (blk, s), (other, 0), keep_self)
        score(sims[:, SEQ:], (blk, s), (other + 1, 0))

    @pl.loop(0, 2 * CHUNKS)
    def _(t):
        @pl.when(t < CHUNKS)
        def _():
            q = t
            landed(slot(M1, 0, q), unit_sem.at[M1, 0, q])
            pass_on((M1, 0), (M2, 0), q, up)
            landed(slot(P1, 0, q), unit_sem.at[P1, 0, q])
            pass_on((P1, 0), (P2, 0), q, down)
            pass_on((P1, 0), (C1, 0), q, across)
            pass_on((M1, 0), (M1, 1), q, mate)

        @pl.when(t >= CHUNKS)
        def _():
            q = t - CHUNKS
            landed(slot(P2, 0, q), unit_sem.at[P2, 0, q])
            pass_on((P2, 0), (C2, 0), q, across)
            landed(slot(M2, 0, q), unit_sem.at[M2, 0, q])
            pass_on((M2, 0), (M2, 1), q, mate)

        @pl.when(t == 2)
        def _():
            for blk, s in USED:
                landed(tokw.at[blk, s], tokw_sem.at[blk, s])

        for when, blk, s in ((4, OWN, 1), (5, C1, 0), (6, M1, 1)):
            @pl.when(t == when)
            def _(blk=blk, s=s):
                all_landed(blk, s)

        @pl.when(t >= 3)
        def _():
            left = jnp.where(t <= 4, OWN, jnp.where(t <= 6, M1, M2))
            sample = jnp.where((t == 4) | (t == 6), 1, 0)
            double(left, sample, jnp.where(t <= 4, OWN, P1), t >= 5)

    @pl.loop(0, 3)
    def _(t):
        single(jnp.where(t < 2, OWN, P1), t % 2, C1)

    all_landed(M2, 1)
    double(M2, 1, P1)

    single(M2, y // 4, P2)

    def send_results(blocks):
        for k, (blk, s) in enumerate(USED):
            if blk in blocks:
                remote(
                    result.at[blk, s], arrived.at[k], result_send.at[k], result_sem.at[k], owner(blk, s)
                ).start()

    send_results((OWN, M1, P1, C1))

    @pl.loop(0, CHUNKS)
    def _(q):
        for m, (src, _) in enumerate(moves):
            sent(slot(*src, q), unit_send.at[m, q])

    all_landed(C2, 0)
    single(M2, 0, C2)
    send_results((M2, P2, C2))
    store.wait()
    for k, (blk, s) in enumerate(USED):
        sent(result.at[blk, s], result_send.at[k])
    for k in range(len(USED)):
        landed(arrived.at[k], result_sem.at[k])
    everything = result[OWN, 0]
    for k in range(len(USED)):
        everything = everything + arrived[k]
    precision = everything[0:1]
    recall = everything[1:2]
    f_score = 2.0 * precision * recall / jnp.maximum(precision + recall, 0.25)
    others = jnp.where((lane < 32) & (lane != number(OWN, 0)), f_score, 0.0)
    utility = jnp.sum(others, axis=1, keepdims=True) / 31.0
    scores_out[...] = jnp.where(line < 2, everything, jnp.where(line == 2, f_score, utility))


def hand_out(
    embedded_ref, scores_ref, embedded_out, precision_out, recall_out, f_out, utility_out,
    emb, scores, row_p, row_r, row_f, one, load_sem, store_sem, small_sem,
):
    parts = emb.shape[0]
    rows = emb.shape[1]
    loads = [
        pltpu.make_async_copy(embedded_ref.at[0, pl.ds(k * rows, rows)], emb.at[k], load_sem.at[k])
        for k in range(parts)
    ]
    stores = [
        pltpu.make_async_copy(emb.at[k], embedded_out.at[0, pl.ds(k * rows, rows)], store_sem.at[k])
        for k in range(parts)
    ]
    load_scores = pltpu.make_async_copy(scores_ref, scores, load_sem.at[parts])
    load_scores.start()
    for load in loads:
        load.start()
    load_scores.wait()
    row_p[...] = scores[0:1, :32]
    row_r[...] = scores[1:2, :32]
    row_f[...] = scores[2:3, :32]
    one[...] = scores[3:4, :1]
    small = [
        pltpu.make_async_copy(src, dst, small_sem.at[k])
        for k, (src, dst) in enumerate(
            ((row_p, precision_out), (row_r, recall_out), (row_f, f_out), (one, utility_out))
        )
    ]
    for copy in small:
        copy.start()
    for load, store in zip(loads, stores):
        load.wait()
        store.start()
    for copy in small + stores:
        copy.wait()


def local(
    context, hidden, out_weight, out_bias, norm_gain, norm_bias, token_ids, lengths, idf_table
):
    vocab = idf_table.shape[0]
    table_rows = vocab // WIDTH * 8 + 16
    vmem = pl.BlockSpec(memory_space=pltpu.VMEM)
    hbm = pl.BlockSpec(memory_space=pl.ANY)
    dma = pltpu.SemaphoreType.DMA
    count = len(USED)
    embedded, scores = pl.pallas_call(
        kernel,
        out_shape=(
            jax.ShapeDtypeStruct((1, SEQ, WIDTH), BF16),
            jax.ShapeDtypeStruct((8, SEQ), F32),
        ),
        in_specs=[hbm] * 9,
        out_specs=(hbm, vmem),
        scratch_shapes=[
            pltpu.VMEM((2, SEQ, WIDTH), BF16),
            pltpu.VMEM((SEQ, WIDTH), BF16),
            pltpu.VMEM((SLOTS, SEQ, WIDTH), BF16),
            pltpu.VMEM((SLOTS, SEQ, SEQ), F32),
            pltpu.VMEM((SEQ, WIDTH), F32),
            pltpu.VMEM((3, 1, WIDTH), F32),
            pltpu.VMEM((1, SEQ), jnp.int32),
            pltpu.SMEM((1,), jnp.int32),
            pltpu.VMEM((vocab,), BF16),
            pltpu.VMEM((table_rows, SEQ), BF16),
            pltpu.VMEM((SEQ, WIDTH), BF16),
            pltpu.VMEM((7, 2, SEQ, WIDTH), BF16),
            pltpu.VMEM((1, WIDTH), F32),
            pltpu.VMEM((7, 2, 8, SEQ), F32),
            pltpu.VMEM((7, 2, 8, SEQ), F32),
            pltpu.VMEM((count, 8, SEQ), F32),
            dma((8,)),
            dma,
            dma((2, 2)),
            dma((SLOTS - 1, PIECES)),
            dma((SLOTS, PIECES)),
            dma((SLOTS - 1, PIECES // 2)),
            dma,
            dma((SLOTS,)),
            dma((count,)),
            dma((9, CHUNKS)),
            dma((count,)),
            dma((SLOTS, PIECES)),
            dma((SLOTS, PIECES)),
            dma,
            dma((SLOTS,)),
            dma((7, 2)),
            dma((7, 2, CHUNKS)),
            dma((count,)),
        ],
        compiler_params=pltpu.CompilerParams(
            collective_id=0, has_side_effects=True, vmem_limit_bytes=60 * 1024 * 1024
        ),
        cost_estimate=pl.CostEstimate(flops=1 << 30, bytes_accessed=1 << 20, transcendentals=0),
    )(
        context, hidden, out_weight.T, out_bias.reshape(1, WIDTH), norm_gain.reshape(1, WIDTH),
        norm_bias.reshape(1, WIDTH), token_ids, lengths, idf_table,
    )
    embedded, precision, recall, f_score, utility = pl.pallas_call(
        hand_out,
        out_shape=(
            jax.ShapeDtypeStruct((1, SEQ, WIDTH), BF16),
            jax.ShapeDtypeStruct((1, 32), F32),
            jax.ShapeDtypeStruct((1, 32), F32),
            jax.ShapeDtypeStruct((1, 32), F32),
            jax.ShapeDtypeStruct((1, 1), F32),
        ),
        in_specs=[hbm, hbm],
        out_specs=(hbm,) * 5,
        scratch_shapes=[
            pltpu.VMEM((2, SEQ // 2, WIDTH), BF16),
            pltpu.VMEM((8, SEQ), F32),
            pltpu.VMEM((1, 32), F32),
            pltpu.VMEM((1, 32), F32),
            pltpu.VMEM((1, 32), F32),
            pltpu.VMEM((1, 1), F32),
            dma((3,)),
            dma((2,)),
            dma((4,)),
        ],
        compiler_params=pltpu.CompilerParams(vmem_limit_bytes=60 * 1024 * 1024),
    )(embedded, scores)
    return embedded, precision, recall, f_score, utility.reshape(1)


def solution(mesh):
    placed = (
        P(("doc", "samp", "tok"), None, None),
        P(("doc", "samp", "tok"), None, None),
        P(None, ("samp", "tok")),
        P(),
        P(),
        P(),
        P(("doc", "samp", "tok"), None),
        P(("doc", "samp", "tok")),
        P(),
    )
    return jax.shard_map(
        local,
        mesh=mesh,
        in_specs=placed,
        out_specs=(
            P(("doc", "samp", "tok"), None, None),
            P(("doc", "samp", "tok"), None),
            P(("doc", "samp", "tok"), None),
            P(("doc", "samp", "tok"), None),
            P(("doc", "samp", "tok")),
        ),
        check_vma=False,
    )
```

```python
import jax
import jax.numpy as jnp
from jax import lax
from jax.experimental import pallas as pl
from jax.experimental.pallas import tpu as pltpu
from jax.sharding import PartitionSpec as P

MESH = pl.DeviceIdType.MESH
F32 = jnp.float32
BF16 = jnp.bfloat16

SEQ = 128
WIDTH = 1024
RING = 8
SLICE = 32
SLOTS = 4
PIECE = 16
PIECES = 2 * SLICE // PIECE
CHUNKS = 4
ROWS = SEQ // CHUNKS
NT = (((1,), (1,)), ((), ()))

OWN, M1, M2, P1, C1, P2, C2 = range(7)
PLACES = {OWN: (0, 0), M1: (-1, 0), M2: (-2, 0), P1: (1, 0), C1: (1, 1), P2: (2, 0), C2: (2, 1)}
USED = [(OWN, 1), (M1, 0), (M1, 1), (M2, 0), (M2, 1), (P1, 0), (C1, 0), (P2, 0), (C2, 0)]


def kernel(
    context_hbm, hidden_hbm, weight_hbm, bias_hbm, gain_hbm, shift_hbm, ids_hbm, length_hbm, table_hbm,
    embedded_out, scores_out,
    ctx, hid, wt, part, mixed, params, ids_ref, length_ref, flat, table, emb, units, first_unit, tokw, result, arrived,
    load_sem, store_sem, first_sem, chain_send, z_send, side_send, ctx_send, part_send, tokw_send, unit_send, result_send,
    slice_sem, z_sem, ctx_sem, part_sem, tokw_sem, unit_sem, result_sem,
):
    doc = lax.axis_index("doc")
    y = lax.axis_index("samp")
    tok = lax.axis_index("tok")
    z, c = tok // 2, tok % 2

    def device(dy, flip_z, flip_c):
        yy = (y + dy + RING) % RING
        zz = 1 - z if flip_z else z
        return (doc, yy, zz * 2 + (c + flip_c) % 2)

    def holder(blk, s):
        dy, flip_z = PLACES[blk]
        return device(-dy, flip_z, s + (1 - z if flip_z else 0))

    def owner(blk, s):
        dy, flip_z = PLACES[blk]
        return device(dy, flip_z, s + (z if flip_z else 0))

    def number(blk, s):
        dy = jnp.where(blk <= M2, -blk, (blk - 1) // 2)
        flip = jnp.where((blk == C1) | (blk == C2), 1, 0)
        return (y + dy + RING) % RING * 4 + (z + flip) % 2 * 2 + (c + s + flip * z) % 2

    up, down, inner, mate = device(1, 0, 0), device(-1, 0, 0), device(0, 1, 0), device(0, 0, 1)
    ahead = device(1 - 2 * c, 0, 0)
    across = device(0, 1, 1 - z)

    def rows_of(zz, piece):
        return pl.ds(pl.multiple_of(zz * 2 * SLICE + piece * PIECE, PIECE), PIECE)

    def own_piece(h):
        return weight_hbm.at[pl.ds(h * PIECE, PIECE)], wt.at[0, rows_of(z, c * 2 + h)]

    @pl.when(c == 0)
    def _():
        for h in (0, 1):
            pltpu.make_async_copy(*own_piece(h), slice_sem.at[0, h]).start()

    loads = [
        pltpu.make_async_copy(context_hbm.at[0], ctx.at[0], load_sem.at[0]),
        pltpu.make_async_copy(table_hbm, flat, load_sem.at[1]),
        pltpu.make_async_copy(ids_hbm, ids_ref, load_sem.at[2]),
        pltpu.make_async_copy(length_hbm, length_ref, load_sem.at[3]),
        pltpu.make_async_copy(hidden_hbm.at[0], hid, load_sem.at[4]),
        pltpu.make_async_copy(bias_hbm, params.at[0], load_sem.at[5]),
        pltpu.make_async_copy(gain_hbm, params.at[1], load_sem.at[6]),
        pltpu.make_async_copy(shift_hbm, params.at[2], load_sem.at[7]),
    ]
    for load in loads:
        load.start()

    partners = [inner, device(0, 1, 1), mate]
    partners += [device(dy, 0, fc) for dy in (1, -1, 2, -2) for fc in (0, 1)]
    partners += [device(dy, 1, z) for dy in (1, 2)]
    partners += [device(dy, 1, 1 - z) for dy in (-1, -2)]
    barrier = pltpu.get_barrier_semaphore()
    for partner in partners:
        pl.semaphore_signal(barrier, inc=1, device_id=partner, device_id_type=MESH)

    def remote(src, dst, send_sem, recv_sem, target):
        return pltpu.make_async_remote_copy(
            src_ref=src, dst_ref=dst, send_sem=send_sem, recv_sem=recv_sem,
            device_id=target, device_id_type=MESH,
        )

    def landed(dst, recv_sem):
        remote(dst, dst, ctx_send, recv_sem, mate).wait_recv()

    def sent(src, send_sem):
        remote(src, src, send_sem, ctx_sem, mate).wait_send()

    result[...] = jnp.zeros_like(result)
    pl.semaphore_wait(barrier, len(partners))

    below = (doc, (y + RING - 1) % RING, z * 2 + 1)

    for h in (0, 1):
        @pl.when(c == 0)
        def _(h=h):
            remote(*own_piece(h), first_sem.at[1, h], slice_sem.at[0, h], below).start()

        @pl.when(c == 1)
        def _(h=h):
            remote(*own_piece(h), first_sem.at[1, h], slice_sem.at[0, 2 + h], below).start()
            remote(*own_piece(h), first_sem.at[0, h], slice_sem.at[0, 2 + h], mate).start()

    loads[0].wait()
    remote(ctx.at[0], ctx.at[1], ctx_send, ctx_sem, mate).start()

    def columns_at(k, core):
        yy = (y + RING + jnp.where(core == 0, -k, k + 1)) % RING
        return pl.ds(pl.multiple_of(yy * SEQ, SEQ), SEQ)

    lane = lax.broadcasted_iota(jnp.int32, (1, SEQ), 1)

    def token_weights():
        for load in loads[1:4]:
            load.wait()
        vocab = flat.shape[0]
        full = vocab // WIDTH
        table[pl.ds(full * 8, 16)] = jnp.zeros((16, SEQ), BF16)

        @pl.loop(0, full)
        def _(k):
            table[pl.ds(pl.multiple_of(k * 8, 8), 8)] = flat[
                pl.ds(pl.multiple_of(k * WIDTH, WIDTH), WIDTH)
            ].reshape(8, SEQ)

        for k in range(full * 8, -(-vocab // SEQ)):
            count = min(SEQ, vocab - k * SEQ)
            table[k:k + 1, :count] = flat[pl.ds(k * SEQ, count)].reshape(1, count)
        ids = ids_ref[...]
        chosen = lax.broadcasted_iota(jnp.int32, (SEQ, SEQ), 0) == (ids & (SEQ - 1))
        columns = jnp.dot(
            table[...], jnp.where(chosen, 1.0, 0.0).astype(BF16), preferred_element_type=F32
        )
        row_hit = lax.broadcasted_iota(jnp.int32, columns.shape, 0) == (ids >> 7)
        found = jnp.sum(jnp.where(row_hit, columns, 0.0), axis=0, keepdims=True)
        own = jnp.where(lane < length_ref[0], found, 0.0)
        own = own / jnp.sum(own, axis=1, keepdims=True)
        tokw[OWN, 0] = jnp.broadcast_to(own, (8, SEQ))
        for k, (blk, s) in enumerate(USED):
            remote(
                tokw.at[OWN, 0], tokw.at[blk, s], tokw_send.at[k], tokw_sem.at[blk, s], holder(blk, s)
            ).start()

    @pl.loop(0, SLOTS + 1)
    def _(k):
        @pl.when(k < SLOTS)
        def _():
            for s in range(PIECES):
                rows = rows_of(z, s)
                landed(wt.at[k, rows], slice_sem.at[k, s])

                @pl.when(k + 1 < SLOTS)
                def _(rows=rows, s=s):
                    remote(
                        wt.at[k, rows], wt.at[k + 1, rows], chain_send.at[k, s], slice_sem.at[k + 1, s], ahead
                    ).start()

                @pl.when((k == 0) | (s < PIECES // 2) | ((k == 3) & (c == 1)))
                def _(rows=rows, s=s):
                    remote(wt.at[k, rows], wt.at[k, rows], z_send.at[k, s], z_sem.at[k, s], inner).start()

        @pl.when(k >= 1)
        def _():
            for s in range(PIECES // 2, PIECES):
                rows = rows_of(1 - z, s)
                landed(wt.at[k - 1, rows], z_sem.at[k - 1, s])

                @pl.when((k < 3) | ((k == 3) & (c == 0)))
                def _(rows=rows, s=s):
                    remote(
                        wt.at[k - 1, rows], wt.at[k, rows], side_send.at[k - 1, s - PIECES // 2], z_sem.at[k, s], ahead
                    ).start()

        @pl.when(k == 3)
        def _():
            landed(ctx.at[1], ctx_sem)

        @pl.when(k >= 3)
        def _():
            first = (k - 3) * 2
            for n in (0, 1):
                for s in range(PIECES // 2):
                    landed(wt.at[first + n, rows_of(1 - z, s)], z_sem.at[first + n, s])
            columns = wt[pl.ds(first, 2)].reshape(2 * SEQ, WIDTH)
            theirs = lax.dot_general(ctx[1], columns, NT, preferred_element_type=F32)
            for n in (0, 1):
                part[first + n] = theirs[:, n * SEQ:(n + 1) * SEQ]
                remote(
                    part.at[first + n], mixed.at[:, columns_at(first + n, c)], part_send.at[first + n],
                    part_sem.at[first + n], mate,
                ).start()
            mine = lax.dot_general(ctx[0], columns, NT, preferred_element_type=F32)
            for n in (0, 1):
                mixed[:, columns_at(first + n, c)] = mine[:, n * SEQ:(n + 1) * SEQ]

        @pl.when(k == 3)
        def _():
            token_weights()

    for load in loads[4:]:
        load.wait()
    for k in range(SLOTS):
        landed(mixed.at[:, columns_at(k, 1 - c)], part_sem.at[k])

    def slot(blk, s, q):
        return units.at[blk, s, pl.ds(pl.multiple_of(q * ROWS, ROWS), ROWS)]

    moves = []

    def pass_on(src, dst, q, target):
        if (src, dst) not in moves:
            moves.append((src, dst))
        remote(
            slot(*src, q), slot(*dst, q), unit_send.at[moves.index((src, dst)), q],
            unit_sem.at[dst[0], dst[1], q], target,
        ).start()

    @pl.loop(0, CHUNKS)
    def _(q):
        rows = pl.ds(pl.multiple_of(q * ROWS, ROWS), ROWS)
        x = hid[rows, :].astype(F32) + mixed[rows, :] + params[0]
        centre = x - jnp.mean(x, axis=-1, keepdims=True)
        spread = jnp.mean(centre * centre, axis=-1, keepdims=True)
        embedded = (centre * lax.rsqrt(spread + 1e-07) * params[1] + params[2]).astype(BF16)
        emb[rows, :] = embedded
        values = embedded.astype(F32)
        unit = values * lax.rsqrt(jnp.sum(values * values, axis=-1, keepdims=True) + 1e-06)

        @pl.when(q == 0)
        def _():
            first_unit[...] = unit[:1]

        real = lax.broadcasted_iota(jnp.int32, (ROWS, 1), 0) + q * ROWS < length_ref[0]
        units[OWN, 0, rows] = jnp.where(real, unit, first_unit[...]).astype(BF16)
        pass_on((OWN, 0), (M1, 0), q, up)
        pass_on((OWN, 0), (P1, 0), q, down)
        pass_on((OWN, 0), (OWN, 1), q, mate)

    store = pltpu.make_async_copy(emb, embedded_out.at[0], store_sem)
    store.start()

    for k in range(SLOTS):
        for s in range(PIECES):
            if k + 1 < SLOTS:
                sent(wt.at[k, rows_of(z, s)], chain_send.at[k, s])
                if k == 2 and s >= PIECES // 2:
                    @pl.when(c == 0)
                    def _(s=s):
                        sent(wt.at[2, rows_of(1 - z, s)], side_send.at[2, s - PIECES // 2])

                    @pl.when(c == 1)
                    def _(s=s):
                        sent(wt.at[3, rows_of(z, s)], z_send.at[3, s])
                elif s >= PIECES // 2:
                    sent(wt.at[k, rows_of(1 - z, s)], side_send.at[k, s - PIECES // 2])
            if k == 0 or s < PIECES // 2:
                sent(wt.at[k, rows_of(z, s)], z_send.at[k, s])
        sent(part.at[k], part_send.at[k])
    sent(ctx.at[0], ctx_send)
    for k in range(len(USED)):
        sent(tokw.at[OWN, 0], tokw_send.at[k])
    for h in (0, 1):
        sent(own_piece(h)[0], first_sem.at[1, h])

    @pl.when(c == 1)
    def _():
        for h in (0, 1):
            sent(own_piece(h)[0], first_sem.at[0, h])

    def all_landed(blk, s):
        for q in range(CHUNKS):
            landed(slot(blk, s, q), unit_sem.at[blk, s, q])

    eye = lax.broadcasted_iota(jnp.int32, (SEQ, SEQ), 0) == lax.broadcasted_iota(jnp.int32, (SEQ, SEQ), 1)
    line = lax.broadcasted_iota(jnp.int32, (8, SEQ), 0)

    def two_lines(first, second):
        return jnp.where(line == 0, first, jnp.where(line == 1, second, 0.0))

    def score(sim, a, b, to_a=True):
        best_a = jnp.sum(jnp.where(eye, jnp.max(sim, axis=1, keepdims=True), 0.0), axis=0, keepdims=True)
        best_b = jnp.max(sim, axis=0, keepdims=True)
        p = jnp.sum(tokw[a[0], a[1], 0:1] * best_a, axis=1, keepdims=True)
        r = jnp.sum(tokw[b[0], b[1], 0:1] * best_b, axis=1, keepdims=True)
        lane_b = number(*b) if to_a is True else jnp.where(to_a, number(*b), -1)
        lane_a = number(*a)
        result[a[0], a[1]] = result[a[0], a[1]] + jnp.where(lane == lane_b, two_lines(p, r), 0.0)
        result[b[0], b[1]] = result[b[0], b[1]] + jnp.where(lane == lane_a, two_lines(r, p), 0.0)

    def single(blk, s, other):
        score(
            lax.dot_general(units[blk, s], units[other, 0], NT, preferred_element_type=F32), (blk, s), (other, 0)
        )

    def double(blk, s, other, keep_self=True):
        sims = lax.dot_general(
            units[blk, s], units[pl.ds(other, 2), 0].reshape(2 * SEQ, WIDTH), NT, preferred_element_type=F32
        )
        score(sims[:, :SEQ], (blk, s), (other, 0), keep_self)
        score(sims[:, SEQ:], (blk, s), (other + 1, 0))

    @pl.loop(0, 2 * CHUNKS)
    def _(t):
        @pl.when(t < CHUNKS)
        def _():
            q = t
            landed(slot(M1, 0, q), unit_sem.at[M1, 0, q])
            pass_on((M1, 0), (M2, 0), q, up)
            landed(slot(P1, 0, q), unit_sem.at[P1, 0, q])
            pass_on((P1, 0), (P2, 0), q, down)
            pass_on((P1, 0), (C1, 0), q, across)
            pass_on((M1, 0), (M1, 1), q, mate)

        @pl.when(t >= CHUNKS)
        def _():
            q = t - CHUNKS
            landed(slot(P2, 0, q), unit_sem.at[P2, 0, q])
            pass_on((P2, 0), (C2, 0), q, across)
            landed(slot(M2, 0, q), unit_sem.at[M2, 0, q])
            pass_on((M2, 0), (M2, 1), q, mate)

        @pl.when(t == 2)
        def _():
            for blk, s in USED:
                landed(tokw.at[blk, s], tokw_sem.at[blk, s])

        for when, blk, s in ((4, OWN, 1), (5, C1, 0), (6, M1, 1)):
            @pl.when(t == when)
            def _(blk=blk, s=s):
                all_landed(blk, s)

        @pl.when(t >= 3)
        def _():
            left = jnp.where(t <= 4, OWN, jnp.where(t <= 6, M1, M2))
            sample = jnp.where((t == 4) | (t == 6), 1, 0)
            double(left, sample, jnp.where(t <= 4, OWN, P1), t >= 5)

    @pl.loop(0, 3)
    def _(t):
        single(jnp.where(t < 2, OWN, P1), t % 2, C1)

    all_landed(M2, 1)
    double(M2, 1, P1)

    single(M2, y // 4, P2)

    def send_results(blocks):
        for k, (blk, s) in enumerate(USED):
            if blk in blocks:
                remote(
                    result.at[blk, s], arrived.at[k], result_send.at[k], result_sem.at[k], owner(blk, s)
                ).start()

    send_results((OWN, M1, P1, C1))

    @pl.loop(0, CHUNKS)
    def _(q):
        for m, (src, _) in enumerate(moves):
            sent(slot(*src, q), unit_send.at[m, q])

    all_landed(C2, 0)
    single(M2, 0, C2)
    send_results((M2, P2, C2))
    store.wait()
    for k, (blk, s) in enumerate(USED):
        sent(result.at[blk, s], result_send.at[k])
    for k in range(len(USED)):
        landed(arrived.at[k], result_sem.at[k])
    everything = result[OWN, 0]
    for k in range(len(USED)):
        everything = everything + arrived[k]
    precision = everything[0:1]
    recall = everything[1:2]
    f_score = 2.0 * precision * recall / jnp.maximum(precision + recall, 0.25)
    others = jnp.where((lane < 32) & (lane != number(OWN, 0)), f_score, 0.0)
    utility = jnp.sum(others, axis=1, keepdims=True) / 31.0
    scores_out[...] = jnp.where(line < 2, everything, jnp.where(line == 2, f_score, utility))


def hand_out(
    embedded_ref, scores_ref, embedded_out, precision_out, recall_out, f_out, utility_out,
    emb, scores, row_p, row_r, row_f, one, load_sem, store_sem, small_sem,
):
    parts = emb.shape[0]
    rows = emb.shape[1]
    loads = [
        pltpu.make_async_copy(embedded_ref.at[0, pl.ds(k * rows, rows)], emb.at[k], load_sem.at[k])
        for k in range(parts)
    ]
    stores = [
        pltpu.make_async_copy(emb.at[k], embedded_out.at[0, pl.ds(k * rows, rows)], store_sem.at[k])
        for k in range(parts)
    ]
    load_scores = pltpu.make_async_copy(scores_ref, scores, load_sem.at[parts])
    load_scores.start()
    for load in loads:
        load.start()
    load_scores.wait()
    row_p[...] = scores[0:1, :32]
    row_r[...] = scores[1:2, :32]
    row_f[...] = scores[2:3, :32]
    one[...] = scores[3:4, :1]
    small = [
        pltpu.make_async_copy(src, dst, small_sem.at[k])
        for k, (src, dst) in enumerate(
            ((row_p, precision_out), (row_r, recall_out), (row_f, f_out), (one, utility_out))
        )
    ]
    for copy in small:
        copy.start()
    for load, store in zip(loads, stores):
        load.wait()
        store.start()
    for copy in small + stores:
        copy.wait()


def local(
    context, hidden, out_weight, out_bias, norm_gain, norm_bias, token_ids, lengths, idf_table
):
    vocab = idf_table.shape[0]
    table_rows = vocab // WIDTH * 8 + 16
    vmem = pl.BlockSpec(memory_space=pltpu.VMEM)
    hbm = pl.BlockSpec(memory_space=pl.ANY)
    dma = pltpu.SemaphoreType.DMA
    count = len(USED)
    embedded, scores = pl.pallas_call(
        kernel,
        out_shape=(
            jax.ShapeDtypeStruct((1, SEQ, WIDTH), BF16),
            jax.ShapeDtypeStruct((8, SEQ), F32),
        ),
        in_specs=[hbm] * 9,
        out_specs=(hbm, vmem),
        scratch_shapes=[
            pltpu.VMEM((2, SEQ, WIDTH), BF16),
            pltpu.VMEM((SEQ, WIDTH), BF16),
            pltpu.VMEM((SLOTS, SEQ, WIDTH), BF16),
            pltpu.VMEM((SLOTS, SEQ, SEQ), F32),
            pltpu.VMEM((SEQ, WIDTH), F32),
            pltpu.VMEM((3, 1, WIDTH), F32),
            pltpu.VMEM((1, SEQ), jnp.int32),
            pltpu.SMEM((1,), jnp.int32),
            pltpu.VMEM((vocab,), BF16),
            pltpu.VMEM((table_rows, SEQ), BF16),
            pltpu.VMEM((SEQ, WIDTH), BF16),
            pltpu.VMEM((7, 2, SEQ, WIDTH), BF16),
            pltpu.VMEM((1, WIDTH), F32),
            pltpu.VMEM((7, 2, 8, SEQ), F32),
            pltpu.VMEM((7, 2, 8, SEQ), F32),
            pltpu.VMEM((count, 8, SEQ), F32),
            dma((8,)),
            dma,
            dma((2, 2)),
            dma((SLOTS - 1, PIECES)),
            dma((SLOTS, PIECES)),
            dma((SLOTS - 1, PIECES // 2)),
            dma,
            dma((SLOTS,)),
            dma((count,)),
            dma((9, CHUNKS)),
            dma((count,)),
            dma((SLOTS, PIECES)),
            dma((SLOTS, PIECES)),
            dma,
            dma((SLOTS,)),
            dma((7, 2)),
            dma((7, 2, CHUNKS)),
            dma((count,)),
        ],
        compiler_params=pltpu.CompilerParams(
            collective_id=0, has_side_effects=True, vmem_limit_bytes=60 * 1024 * 1024
        ),
        cost_estimate=pl.CostEstimate(flops=1 << 30, bytes_accessed=1 << 20, transcendentals=0),
    )(
        context, hidden, out_weight.T, out_bias.reshape(1, WIDTH), norm_gain.reshape(1, WIDTH),
        norm_bias.reshape(1, WIDTH), token_ids, lengths, idf_table,
    )
    embedded, precision, recall, f_score, utility = pl.pallas_call(
        hand_out,
        out_shape=(
            jax.ShapeDtypeStruct((1, SEQ, WIDTH), BF16),
            jax.ShapeDtypeStruct((1, 32), F32),
            jax.ShapeDtypeStruct((1, 32), F32),
            jax.ShapeDtypeStruct((1, 32), F32),
            jax.ShapeDtypeStruct((1, 1), F32),
        ),
        in_specs=[hbm, hbm],
        out_specs=(hbm,) * 5,
        scratch_shapes=[
            pltpu.VMEM((2, SEQ // 2, WIDTH), BF16),
            pltpu.VMEM((8, SEQ), F32),
            pltpu.VMEM((1, 32), F32),
            pltpu.VMEM((1, 32), F32),
            pltpu.VMEM((1, 32), F32),
            pltpu.VMEM((1, 1), F32),
            dma((3,)),
            dma((2,)),
            dma((4,)),
        ],
        compiler_params=pltpu.CompilerParams(vmem_limit_bytes=60 * 1024 * 1024),
    )(embedded, scores)
    return embedded, precision, recall, f_score, utility.reshape(1)


def solution(mesh):
    placed = (
        P(("doc", "samp", "tok"), None, None),
        P(("doc", "samp", "tok"), None, None),
        P(None, ("samp", "tok")),
        P(),
        P(),
        P(),
        P(("doc", "samp", "tok"), None),
        P(("doc", "samp", "tok")),
        P(),
    )
    return jax.shard_map(
        local,
        mesh=mesh,
        in_specs=placed,
        out_specs=(
            P(("doc", "samp", "tok"), None, None),
            P(("doc", "samp", "tok"), None),
            P(("doc", "samp", "tok"), None),
            P(("doc", "samp", "tok"), None),
            P(("doc", "samp", "tok")),
        ),
        check_vma=False,
    )
```
